32 devices in a mesh: gy: 8 (over z, core), gx: 4 (over y, x).
Axes of the slice: x: 2, y: 2, z: 4, core: 2. Of those that a mesh axis runs over, the one named last changes fastest.
Arguments:
- features: bfloat16 [512, 64, 128], P('gy', 'gx'), may hold values from -40 to 40
- attention_gain: float32 [2, 128], replicated, may hold values from 0.25 to 1.75
- triple_weight: bfloat16 [2, 128, 384], replicated, may hold values from -0.5 to 0.5
- output_weight: bfloat16 [2, 128, 128], replicated, may hold values from -0.5 to 0.5
- position_bias: float32 [2, 4, 225], replicated, may hold values from -2 to 262
- hidden_gain: float32 [2, 128], replicated, may hold values from 0.25 to 1.75
- expand_weight: bfloat16 [2, 128, 512], replicated, may hold values from -0.5 to 0.5
- shrink_weight: bfloat16 [2, 512, 128], replicated, may hold values from -0.25 to 0.25
Outputs:
- result: float32 [512, 64, 128], P('gy', 'gx')
The draws below stay inside these ranges and needn't reach their ends.
All inputs are finite; a program needn't handle non-finite values.
Results may differ from the reference program's by a relative error of at most 0.0033.
Values may be sent and summed in bfloat16 or wider, within the bound.
A program may use at most 64 MiB of HBM per device.

```python
import math
import jax
import jax.numpy as jnp
from jax import lax

C = 128
HEADS = 4
HID = 512
WIN = 8
HD = 32
SHIFT = 4
ROWS = 512
COLS = 64


def draw_features(key, part):
    key = jax.random.fold_in(key, 5)
    subkeys = jax.random.split(key, 3)
    channel_scale = jnp.exp(jax.random.uniform(subkeys[0], (C,), jnp.float32, 0.0, math.log(10.0)))
    token_scale = jnp.exp(jax.random.uniform(subkeys[1], (ROWS, COLS, 1), jnp.float32, 0.0, math.log(10.0)))
    raw_values = jax.random.truncated_normal(subkeys[2], -4.0, 4.0, (ROWS, COLS, C), jnp.float32)
    return (0.1 * raw_values * channel_scale * token_scale).astype(jnp.bfloat16)


def draw_position_bias(key, part):
    key = jax.random.fold_in(key, 9)
    subkeys = jax.random.split(key, 1)
    extent = 2 * WIN - 1
    values_table = jax.random.uniform(subkeys[0], (2, HEADS, extent * extent), jnp.float32, -2.0, 2.0)
    return values_table


def centred(key, dims, deviation, most, held_as=jnp.bfloat16):
    return jnp.clip(deviation * jax.random.normal(key, dims, jnp.float32), -most, most).astype(held_as)


def setup_inputs(seed: int = 0) -> dict:
    key_of = jax.random.split(jax.random.key(seed), 9)
    return {
        "features": draw_features(jax.random.fold_in(key_of[8], 71), 0),
        "attention_gain": jnp.clip(1.0 + 0.15 * jax.random.normal(key_of[1], (2, C), jnp.float32), 0.25, 1.75),
        "triple_weight": centred(key_of[2], (2, C, 3 * C), C ** -0.5, 0.5),
        "output_weight": centred(key_of[3], (2, C, C), C ** -0.5, 0.5),
        "position_bias": draw_position_bias(jax.random.fold_in(key_of[8], 71), 0),
        "hidden_gain": jnp.clip(1.0 + 0.15 * jax.random.normal(key_of[5], (2, C), jnp.float32), 0.25, 1.75),
        "expand_weight": centred(key_of[6], (2, C, HID), C ** -0.5, 0.5),
        "shrink_weight": centred(key_of[7], (2, HID, C), HID ** -0.5, 0.25),
    }


EPSILON = 1e-05

def layer_norm(values, gain_vector):
    center = values - lax.optimization_barrier(jnp.mean(values, axis=-1, keepdims=True))
    spread = lax.optimization_barrier(jnp.mean(center * center, axis=-1, keepdims=True))
    return (center * lax.rsqrt(spread + EPSILON) * gain_vector).astype(jnp.bfloat16)

def window_attention(triple, band_labels, bias_block, out_weight):
    breadth = triple.shape[1]
    windows = breadth // WIN
    pieces = triple.reshape(WIN, windows, WIN, 3, HEADS, HD).transpose(3, 1, 4, 0, 2, 5)
    pieces = pieces.reshape(3, windows, HEADS, WIN * WIN, HD).astype(jnp.float32)
    scores = jnp.einsum('whqd,whkd->whqk', pieces[0], pieces[1]) * HD ** (-0.5) + bias_block[None]
    labels_win = band_labels.reshape(WIN, windows, WIN).transpose(1, 0, 2).reshape(windows, WIN * WIN)
    scores = scores + jnp.where(labels_win[:, None, :, None] != labels_win[:, None, None, :], -100.0, 0.0).astype(jnp.float32)
    row_max = lax.optimization_barrier(jnp.max(scores, axis=-1, keepdims=True))
    powers = jnp.exp(scores - row_max)
    probabilities = (powers / lax.optimization_barrier(jnp.sum(powers, axis=-1, keepdims=True))).astype(jnp.bfloat16)
    context = jnp.einsum('whqk,whkd->whqd', probabilities.astype(jnp.float32), pieces[2]).astype(jnp.bfloat16)
    context = context.reshape(windows, HEADS, WIN, WIN, HD).transpose(2, 0, 3, 1, 4).reshape(WIN * breadth, C)
    branch = jnp.dot(context, out_weight, preferred_element_type=jnp.float32).astype(jnp.bfloat16)
    return branch.reshape(WIN, breadth, C)

def reference(features, attention_gain, triple_weight, output_weight, position_bias, hidden_gain, expand_weight, shrink_weight):
    extent = 2 * WIN - 1
    places = jnp.arange(WIN * WIN, dtype=jnp.int32)
    along_y = places // WIN
    along_x = places % WIN
    offset = (along_y[:, None] - along_y[None, :] + WIN - 1) * extent + along_x[:, None] - along_x[None, :] + WIN - 1
    tables = position_bias[:, :, offset]

    def run_block(inputs, labels, block_index):

        def one_band(packed):
            band_values, band_labels = packed
            normed = layer_norm(band_values, attention_gain[block_index])
            triple = jnp.dot(normed.reshape(-1, C), triple_weight[block_index], preferred_element_type=jnp.float32)
            triple = triple.astype(jnp.bfloat16).reshape(WIN, COLS, 3 * C)
            branch = window_attention(triple, band_labels, tables[block_index], output_weight[block_index])
            middle = band_values + branch.astype(jnp.float32)
            normed_mid = layer_norm(middle, hidden_gain[block_index])
            hidden = jax.nn.gelu(jnp.dot(normed_mid.reshape(-1, C), expand_weight[block_index], preferred_element_type=jnp.float32), approximate=False).astype(jnp.bfloat16)
            return middle + jnp.dot(hidden, shrink_weight[block_index], preferred_element_type=jnp.float32).reshape(WIN, COLS, C)
        outputs = lax.map(one_band, (inputs.reshape(ROWS // WIN, WIN, COLS, C), labels.reshape(ROWS // WIN, WIN, COLS)))
        return outputs.reshape(ROWS, COLS, C)
    first_out = run_block(features.astype(jnp.float32), jnp.zeros((ROWS, COLS), jnp.int32), 0)
    frame_rows = jnp.arange(ROWS, dtype=jnp.int32)
    frame_cols = jnp.arange(COLS, dtype=jnp.int32)
    row_label = (frame_rows >= ROWS - WIN).astype(jnp.int32) + (frame_rows >= ROWS - SHIFT).astype(jnp.int32)
    col_label = (frame_cols >= COLS - WIN).astype(jnp.int32) + (frame_cols >= COLS - SHIFT).astype(jnp.int32)
    labels = row_label[:, None] * 3 + col_label[None, :]
    rolled = jnp.roll(first_out, (-SHIFT, -SHIFT), axis=(0, 1))
    second = run_block(rolled, labels, 1)
    return jnp.roll(second, (SHIFT, SHIFT), axis=(0, 1))
```

```python
import functools

import jax
import jax.numpy as jnp
from jax import lax
from jax.experimental import pallas as pl
from jax.experimental.pallas import tpu as pltpu
from jax.sharding import PartitionSpec as P

C = 128
HEADS = 4
WIN = 8
HD = 32
SHIFT = 4
EPSILON = 1e-05
F32 = jnp.float32
BF16 = jnp.bfloat16
GROUP = 2


def layer_norm(values, gain):
    center = values - jnp.mean(values, axis=-1, keepdims=True)
    spread = jnp.mean(center * center, axis=-1, keepdims=True)
    return center * lax.rsqrt(spread + EPSILON) * gain


def gelu(x):
    a = jnp.abs(x)
    t = 1.0 / (1.0 + (0.3275911 * 0.5**0.5) * a)
    poly = 0.5 * 1.061405429
    for coef in (-1.453152027, 1.421413741, -0.284496736, 0.254829592):
        poly = poly * t + 0.5 * coef
    tail = poly * t * jnp.exp(-0.5 * (a * a))
    return jnp.maximum(x, 0.0) - a * tail


def window_pair(triple, bias, second, heads):
    triple = triple.reshape(WIN, 2 * WIN, 3 * C)
    query = triple[:, :, :C].reshape(2 * WIN * WIN, C)
    zero = jnp.zeros_like(query)
    query = jnp.concatenate(
        [jnp.where(second, zero, query), jnp.where(second, query, zero)], axis=1
    ).astype(BF16)
    keys, values = [], []
    for w in range(2):
        part = triple[:, w * WIN : (w + 1) * WIN, C:].reshape(WIN * WIN, 2 * C).astype(BF16)
        keys.append(jnp.concatenate([part[:, :C] * m for m in heads], axis=0))
        values.append(jnp.concatenate([part[:, C:] * m for m in heads], axis=0))
    keys = jnp.concatenate(keys, axis=1)
    values = jnp.concatenate(values, axis=1)
    scores = lax.dot_general(keys, query, (((1,), (1,)), ((), ())), preferred_element_type=F32)
    scores = (scores * HD ** (-0.5) + bias).reshape(HEADS, WIN * WIN, 2 * WIN * WIN)
    powers = jnp.exp(scores - jnp.max(scores, axis=1, keepdims=True))
    probs = powers * (1.0 / jnp.sum(powers, axis=1, keepdims=True))
    probs = probs.reshape(HEADS * WIN * WIN, 2 * WIN * WIN).astype(BF16)
    both = lax.dot_general(probs, values, (((0,), (0,)), ((), ())), preferred_element_type=F32)
    return jnp.where(second, both[:, C:], both[:, :C]).astype(BF16)


def kernel(
    ny, nx, height, breadth,
    feat, again, tw, ow, table, hgain, ew, sw, out,
    first, ext, back, bias, cs, cr, rs, rr, ds, dr, bcs, bcr, brs, brr, bds, bdr, ssem, rsem,
):
    gy, gx = lax.axis_index("gy"), lax.axis_index("gx")
    up, down = lax.rem(gy + ny - 1, ny), lax.rem(gy + 1, ny)
    left, right = lax.rem(gx + nx - 1, nx), lax.rem(gx + 1, nx)
    barrier = pltpu.get_barrier_semaphore()
    around = [(up, gx), (gy, left), (up, left), (down, gx), (gy, right), (down, right)]
    for who in around:
        pl.semaphore_signal(barrier, inc=1, device_id=who, device_id_type=pl.DeviceIdType.MESH)

    jj = lax.broadcasted_iota(jnp.int32, (WIN, 2 * WIN * WIN), 0)
    lane = lax.broadcasted_iota(jnp.int32, (WIN, 2 * WIN * WIN), 1)
    col_cut = ((jj >= SHIFT) != (lane % WIN >= SHIFT)) & (lane % (2 * WIN) >= WIN) & (gx == nx - 1)
    for b in range(2):
        for h in range(HEADS):
            rows = table[b, h]
            for y in range(WIN):
                at = (WIN - 1 - y) * 2 * WIN
                piece = rows[:, at : at + 2 * WIN * WIN]
                spot = slice(h * 64 + y * WIN, h * 64 + (y + 1) * WIN)
                if b == 0:
                    bias[0, spot] = piece
                else:
                    row_cut = ((lane >= SHIFT * 2 * WIN) != (y >= SHIFT)) & (gy == ny - 1)
                    bias[1, spot] = piece + jnp.where(col_cut, -100.0, 0.0)
                    bias[2, spot] = piece + jnp.where(col_cut | row_cut, -100.0, 0.0)

    token = lax.broadcasted_iota(jnp.int32, (2 * WIN * WIN, C), 0)
    second = token % (2 * WIN) >= WIN
    channel = lax.broadcasted_iota(jnp.int32, (1, C), 1)
    heads = [jnp.where(channel // HD == h, 1.0, 0.0).astype(BF16) for h in range(HEADS)]
    bands = height // WIN
    band = 2 * WIN * WIN
    group = GROUP if bands % GROUP == 0 else 1

    def dot(a, b):
        return jnp.dot(a, b, preferred_element_type=F32)

    def spots(i):
        return [i * group + k for k in range(group)]

    def ffn(z, b):
        normed = layer_norm(z, hgain[b : b + 1]).astype(BF16)
        hidden = gelu(dot(normed, ew[b])).astype(BF16)
        return z + dot(hidden, sw[b])

    def block0(i, carry):
        places = spots(i)
        z = jnp.concatenate(
            [feat[pl.ds(r * WIN, WIN), pl.ds(0, 2 * WIN), :].reshape(band, C) for r in places], axis=0
        ).astype(F32)
        triple = dot(layer_norm(z, again[0:1]).astype(BF16), tw[0])
        ctx = [window_pair(triple[k * band : (k + 1) * band], bias[0], second, heads) for k in range(group)]
        branch = dot(jnp.concatenate(ctx, axis=0), ow[0]).astype(BF16).astype(F32)
        z = ffn(z + branch, 0)
        normed = layer_norm(z, again[1:2])
        for k, r in enumerate(places):
            spot = (pl.ds(r * WIN, WIN), pl.ds(0, 2 * WIN), slice(None))
            first[spot] = z[k * band : (k + 1) * band].reshape(WIN, 2 * WIN, C)
            ext[spot] = normed[k * band : (k + 1) * band].reshape(WIN, 2 * WIN, C)
        return carry

    lax.fori_loop(0, bands // group, block0, 0)

    def remote(src, dst, k, who):
        return pltpu.make_async_remote_copy(
            src_ref=src, dst_ref=dst, send_sem=ssem.at[k], recv_sem=rsem.at[k],
            device_id=who, device_id_type=pl.DeviceIdType.MESH,
        )

    half = height // 2

    def pack(ref, r0, c0):
        low = ref[r0 : r0 + half, c0 : c0 + SHIFT, :]
        high = ref[r0 + half : r0 + height, c0 : c0 + SHIFT, :]
        return jnp.concatenate([low, high], axis=1).reshape(half * WIN, C).astype(BF16)

    def unpack(ref, r0, c0, buf):
        both = buf[...].astype(F32).reshape(half, WIN, C)
        ref[r0 : r0 + half, c0 : c0 + SHIFT, :] = both[:, :SHIFT]
        ref[r0 + half : r0 + height, c0 : c0 + SHIFT, :] = both[:, SHIFT:]

    cs[...] = pack(ext, 0, 0)
    rs[...] = ext[0:SHIFT, 0:breadth, :].reshape(SHIFT * breadth, C).astype(BF16)
    ds[...] = ext[0:SHIFT, 0:WIN, :].reshape(SHIFT * WIN, C).astype(BF16)
    pl.semaphore_wait(barrier, 6)
    sends = [remote(cs, cr, 0, (gy, left)), remote(rs, rr, 1, (up, gx)), remote(ds, dr, 2, (up, left))]
    for s in sends:
        s.start()
    for s in sends:
        s.wait()
    unpack(ext, 0, breadth, cr)
    ext[height : height + SHIFT, 0:breadth, :] = rr[...].astype(F32).reshape(SHIFT, breadth, C)
    ext[height : height + SHIFT, breadth : breadth + SHIFT, :] = (
        dr[...].astype(F32).reshape(SHIFT, WIN, C)[:, :SHIFT]
    )

    def block1(i, carry):
        places = spots(i)
        x = jnp.concatenate(
            [
                ext[pl.ds(r * WIN + SHIFT, WIN), pl.ds(SHIFT, 2 * WIN), :].reshape(band, C)
                for r in places
            ],
            axis=0,
        ).astype(BF16)
        triple = dot(x, tw[1])
        ctx = [
            window_pair(
                triple[k * band : (k + 1) * band],
                bias[jnp.where(r == bands - 1, 2, 1)],
                second, heads,
            )
            for k, r in enumerate(places)
        ]
        branch = dot(jnp.concatenate(ctx, axis=0), ow[1])
        for k, r in enumerate(places):
            back[pl.ds(r * WIN + SHIFT, WIN), pl.ds(SHIFT, 2 * WIN), :] = branch[
                k * band : (k + 1) * band
            ].reshape(WIN, 2 * WIN, C)
        return carry

    lax.fori_loop(0, bands // group, block1, 0)

    bcs[...] = pack(back, SHIFT, breadth)
    brs[...] = back[height : height + SHIFT, 0:breadth, :].reshape(SHIFT * breadth, C).astype(BF16)
    bds[...] = back[height : height + SHIFT, breadth : breadth + WIN, :].reshape(SHIFT * WIN, C).astype(BF16)
    sends = [
        remote(bcs, bcr, 3, (gy, right)),
        remote(brs, brr, 4, (down, gx)),
        remote(bds, bdr, 5, (down, right)),
    ]
    for s in sends:
        s.start()
    for s in sends:
        s.wait()
    unpack(back, SHIFT, 0, bcr)
    back[0:SHIFT, 0:breadth, :] = brr[...].astype(F32).reshape(SHIFT, breadth, C)
    back[0:SHIFT, 0:SHIFT, :] = bdr[...].astype(F32).reshape(SHIFT, WIN, C)[:, :SHIFT]

    def tail(i, carry):
        places = spots(i)
        z = jnp.concatenate(
            [
                (
                    first[pl.ds(r * WIN, WIN), pl.ds(0, 2 * WIN), :]
                    + back[pl.ds(r * WIN, WIN), pl.ds(0, 2 * WIN), :].astype(BF16).astype(F32)
                ).reshape(band, C)
                for r in places
            ],
            axis=0,
        )
        z = ffn(z, 1)
        for k, r in enumerate(places):
            out[pl.ds(r * WIN, WIN), pl.ds(0, 2 * WIN), :] = z[k * band : (k + 1) * band].reshape(
                WIN, 2 * WIN, C
            )
        return carry

    lax.fori_loop(0, bands // group, tail, 0)


def bias_rows(position_bias):
    extent = 2 * WIN - 1
    grid = position_bias.reshape(2, HEADS, extent, extent)
    rows = jnp.stack([grid[..., WIN - 1 - x : extent - x] for x in range(WIN)], axis=2)
    rows = jnp.concatenate([rows, rows], axis=-1).reshape(2, HEADS, WIN, extent * 2 * WIN)
    return jnp.pad(rows, ((0, 0), (0, 0), (0, 0), (0, 2 * WIN)))


def on_device(ny, nx, features, attention_gain, triple_weight, output_weight, position_bias,
              hidden_gain, expand_weight, shrink_weight):
    height, breadth, _ = features.shape
    col, row, corner = (height * SHIFT, C), (SHIFT * breadth, C), (SHIFT * WIN, C)
    vmem = pl.BlockSpec(memory_space=pltpu.VMEM)
    return pl.pallas_call(
        functools.partial(kernel, ny, nx, height, breadth),
        out_shape=jax.ShapeDtypeStruct((height, breadth, C), F32),
        in_specs=[vmem] * 8,
        out_specs=vmem,
        scratch_shapes=[
            pltpu.VMEM((height, breadth, C), F32),
            pltpu.VMEM((height + SHIFT, breadth + WIN, C), F32),
            pltpu.VMEM((height + SHIFT, breadth + WIN, C), F32),
            pltpu.VMEM((3, HEADS * WIN * WIN, 2 * WIN * WIN), F32),
        ]
        + [pltpu.VMEM(shape, BF16) for shape in (col, col, row, row, corner, corner)] * 2
        + [pltpu.SemaphoreType.DMA((6,)), pltpu.SemaphoreType.DMA((6,))],
        compiler_params=pltpu.CompilerParams(
            collective_id=0, has_side_effects=True, vmem_limit_bytes=48 * 1024 * 1024
        ),
        cost_estimate=pl.CostEstimate(flops=10**9, bytes_accessed=2 * 10**6, transcendentals=10**6),
    )(features, attention_gain, triple_weight, output_weight, bias_rows(position_bias),
      hidden_gain, expand_weight, shrink_weight)


def solution(mesh):
    return jax.shard_map(
        functools.partial(on_device, mesh.shape["gy"], mesh.shape["gx"]),
        mesh=mesh,
        in_specs=(P("gy", "gx", None), P(), P(), P(), P(), P(), P(), P()),
        out_specs=P("gy", "gx", None),
        check_vma=False,
    )
```

```python
import functools

import jax
import jax.numpy as jnp
from jax import lax
from jax.experimental import pallas as pl
from jax.experimental.pallas import tpu as pltpu
from jax.sharding import PartitionSpec as P

C = 128
HEADS = 4
WIN = 8
HD = 32
SHIFT = 4
EPSILON = 1e-05
F32 = jnp.float32
BF16 = jnp.bfloat16
GROUP = 2


def layer_norm(values, gain):
    center = values - jnp.mean(values, axis=-1, keepdims=True)
    spread = jnp.mean(center * center, axis=-1, keepdims=True)
    return center * lax.rsqrt(spread + EPSILON) * gain


def gelu(x):
    a = jnp.abs(x)
    t = 1.0 / (1.0 + (0.3275911 * 0.5**0.5) * a)
    poly = 0.5 * 1.061405429
    for coef in (-1.453152027, 1.421413741, -0.284496736, 0.254829592):
        poly = poly * t + 0.5 * coef
    tail = poly * t * jnp.exp(-0.5 * (a * a))
    return jnp.maximum(x, 0.0) - a * tail


def window_pair(triple, bias, second, heads):
    triple = triple.reshape(WIN, 2 * WIN, 3 * C)
    query = triple[:, :, :C].reshape(2 * WIN * WIN, C)
    zero = jnp.zeros_like(query)
    query = jnp.concatenate(
        [jnp.where(second, zero, query), jnp.where(second, query, zero)], axis=1
    ).astype(BF16)
    keys, values = [], []
    for w in range(2):
        part = triple[:, w * WIN : (w + 1) * WIN, C:].reshape(WIN * WIN, 2 * C).astype(BF16)
        keys.append(jnp.concatenate([part[:, :C] * m for m in heads], axis=0))
        values.append(jnp.concatenate([part[:, C:] * m for m in heads], axis=0))
    keys = jnp.concatenate(keys, axis=1)
    values = jnp.concatenate(values, axis=1)
    scores = lax.dot_general(keys, query, (((1,), (1,)), ((), ())), preferred_element_type=F32)
    scores = (scores * HD ** (-0.5) + bias).reshape(HEADS, WIN * WIN, 2 * WIN * WIN)
    powers = jnp.exp(scores - jnp.max(scores, axis=1, keepdims=True))
    probs = powers * (1.0 / jnp.sum(powers, axis=1, keepdims=True))
    probs = probs.reshape(HEADS * WIN * WIN, 2 * WIN * WIN).astype(BF16)
    both = lax.dot_general(probs, values, (((0,), (0,)), ((), ())), preferred_element_type=F32)
    return jnp.where(second, both[:, C:], both[:, :C]).astype(BF16)


def kernel(
    ny, nx, height, breadth,
    feat_in, again_in, tw_in, ow_in, table_in, hgain_in, ew_in, sw_in, out_ref,
    feat, again, tw, ow, table, hgain, ew, sw, out,
    first, ext, back, bias, cs, cr, bcs, bcr, rs, rr, brs, brr, ds, dr, bds, bdr,
    ssem, rsem, isem, osem,
):
    loads = [
        pltpu.make_async_copy(src, dst, isem.at[k])
        for k, (src, dst) in enumerate(
            [
                (table_in, table), (feat_in, feat), (again_in, again), (tw_in, tw),
                (ow_in, ow), (hgain_in, hgain), (ew_in, ew), (sw_in, sw),
            ]
        )
    ]
    for load in loads:
        load.start()
    gy, gx = lax.axis_index("gy"), lax.axis_index("gx")
    up, down = lax.rem(gy + ny - 1, ny), lax.rem(gy + 1, ny)
    left, right = lax.rem(gx + nx - 1, nx), lax.rem(gx + 1, nx)
    barrier = pltpu.get_barrier_semaphore()
    around = [(up, gx), (gy, left), (up, left), (down, gx), (gy, right), (down, right)]
    for who in around:
        pl.semaphore_signal(barrier, inc=1, device_id=who, device_id_type=pl.DeviceIdType.MESH)

    jj = lax.broadcasted_iota(jnp.int32, (WIN, 2 * WIN * WIN), 0)
    lane = lax.broadcasted_iota(jnp.int32, (WIN, 2 * WIN * WIN), 1)
    col_cut = ((jj >= SHIFT) != (lane % WIN >= SHIFT)) & (lane % (2 * WIN) >= WIN) & (gx == nx - 1)
    extent = 2 * WIN - 1
    entry = lax.broadcasted_iota(jnp.int32, (extent * extent, 4 * WIN * WIN), 0)
    place = lax.broadcasted_iota(jnp.int32, (extent * extent, 4 * WIN * WIN), 1)
    pick = jnp.where(
        (entry == place // (2 * WIN) * extent + place % (2 * WIN)) & (place % (2 * WIN) < extent), 1.0, 0.0
    )
    first_half = lax.broadcasted_iota(jnp.int32, (WIN, 4 * WIN * WIN), 1) % (2 * WIN) < WIN
    loads[0].wait()
    spread_rows = [
        jnp.dot(table[b], pick, precision=lax.Precision.HIGHEST, preferred_element_type=F32) for b in range(2)
    ]
    for b in range(2):
        for h in range(HEADS):
            row = jnp.broadcast_to(spread_rows[b][h : h + 1], (WIN, 4 * WIN * WIN))
            rows = jnp.where(
                first_half,
                pltpu.roll(row, 4 * WIN * WIN - WIN + 1, 1, stride=1, stride_axis=0),
                pltpu.roll(row, 1, 1, stride=1, stride_axis=0),
            )
            for y in range(WIN):
                at = (WIN - 1 - y) * 2 * WIN
                piece = rows[:, at : at + 2 * WIN * WIN]
                spot = slice(h * 64 + y * WIN, h * 64 + (y + 1) * WIN)
                if b == 0:
                    bias[0, spot] = piece
                else:
                    row_cut = ((lane >= SHIFT * 2 * WIN) != (y >= SHIFT)) & (gy == ny - 1)
                    bias[1, spot] = piece + jnp.where(col_cut, -100.0, 0.0)
                    bias[2, spot] = piece + jnp.where(col_cut | row_cut, -100.0, 0.0)

    token = lax.broadcasted_iota(jnp.int32, (2 * WIN * WIN, C), 0)
    second = token % (2 * WIN) >= WIN
    channel = lax.broadcasted_iota(jnp.int32, (1, C), 1)
    heads = [jnp.where(channel // HD == h, 1.0, 0.0).astype(BF16) for h in range(HEADS)]
    bands = height // WIN
    band = 2 * WIN * WIN
    group = GROUP
    groups = bands // group
    tall = group * WIN

    def dot(a, b):
        return jnp.dot(a, b, preferred_element_type=F32)

    def spots(i):
        return [i * group + k for k in range(group)]

    def ffn(z, b):
        normed = layer_norm(z, hgain[b : b + 1]).astype(BF16)
        hidden = gelu(dot(normed, ew[b])).astype(BF16)
        return z + dot(hidden, sw[b])

    def block0(i, carry):
        places = spots(i)
        z = jnp.concatenate(
            [feat[pl.ds(r * WIN, WIN), pl.ds(0, 2 * WIN), :].reshape(band, C) for r in places], axis=0
        ).astype(F32)
        triple = dot(layer_norm(z, again[0:1]).astype(BF16), tw[0])
        ctx = [window_pair(triple[k * band : (k + 1) * band], bias[0], second, heads) for k in range(group)]
        branch = dot(jnp.concatenate(ctx, axis=0), ow[0]).astype(BF16).astype(F32)
        z = ffn(z + branch, 0)
        normed = layer_norm(z, again[1:2])
        for k, r in enumerate(places):
            spot = (pl.ds(r * WIN, WIN), pl.ds(0, 2 * WIN), slice(None))
            first[spot] = z[k * band : (k + 1) * band].reshape(WIN, 2 * WIN, C)
            ext[spot] = normed[k * band : (k + 1) * band].reshape(WIN, 2 * WIN, C)
        return carry

    def remote(src, dst, k, who):
        return pltpu.make_async_remote_copy(
            src_ref=src, dst_ref=dst, send_sem=ssem.at[k], recv_sem=rsem.at[k],
            device_id=who, device_id_type=pl.DeviceIdType.MESH,
        )

    def column(g):
        return remote(cs.at[g], cr.at[g], g, (gy, left))

    def column_back(g):
        return remote(bcs.at[g], bcr.at[g], groups + g, (gy, right))

    strips = [
        remote(rs, rr, 2 * groups, (up, gx)), remote(ds, dr, 2 * groups + 1, (up, left)),
        remote(brs, brr, 2 * groups + 2, (down, gx)), remote(bds, bdr, 2 * groups + 3, (down, right)),
    ]
    half = tall // 2

    def pack(ref, r0, c0):
        low = ref[pl.ds(r0, half), c0 : c0 + SHIFT, :]
        high = ref[pl.ds(r0 + half, half), c0 : c0 + SHIFT, :]
        return jnp.concatenate([low, high], axis=1).reshape(half * WIN, C).astype(BF16)

    def unpack(ref, r0, c0, buf):
        both = buf.astype(F32).reshape(half, WIN, C)
        ref[pl.ds(r0, half), c0 : c0 + SHIFT, :] = both[:, :SHIFT]
        ref[pl.ds(r0 + half, half), c0 : c0 + SHIFT, :] = both[:, SHIFT:]

    for load in loads[1:]:
        load.wait()

    def step0(i, carry):
        g = lax.rem(groups - i, groups)
        block0(g, carry)
        cs[g] = pack(ext, g * tall, 0)

        @pl.when(i == 0)
        def _():
            rs[...] = ext[0:SHIFT, 0:breadth, :].reshape(SHIFT * breadth, C).astype(BF16)
            ds[...] = ext[0:SHIFT, 0:WIN, :].reshape(SHIFT * WIN, C).astype(BF16)
            pl.semaphore_wait(barrier, 6)
            strips[0].start()
            strips[1].start()

        column(g).start()
        return carry

    lax.fori_loop(0, groups, step0, 0)

    def block1(i, carry):
        places = spots(i)
        x = jnp.concatenate(
            [
                ext[pl.ds(r * WIN + SHIFT, WIN), pl.ds(SHIFT, 2 * WIN), :].reshape(band, C)
                for r in places
            ],
            axis=0,
        ).astype(BF16)
        triple = dot(x, tw[1])
        ctx = [
            window_pair(
                triple[k * band : (k + 1) * band],
                bias[jnp.where(r == bands - 1, 2, 1)],
                second, heads,
            )
            for k, r in enumerate(places)
        ]
        branch = dot(jnp.concatenate(ctx, axis=0), ow[1])
        for k, r in enumerate(places):
            back[pl.ds(r * WIN + SHIFT, WIN), pl.ds(SHIFT, 2 * WIN), :] = branch[
                k * band : (k + 1) * band
            ].reshape(WIN, 2 * WIN, C)
        return carry

    def step1(i, carry):
        g = groups - 1 - i

        @pl.when(i == 0)
        def _():
            strips[0].wait()
            strips[1].wait()
            ext[height : height + SHIFT, 0:breadth, :] = rr[...].astype(F32).reshape(SHIFT, breadth, C)
            ext[height : height + SHIFT, breadth : breadth + SHIFT, :] = (
                dr[...].astype(F32).reshape(SHIFT, WIN, C)[:, :SHIFT]
            )

        column(g).wait()
        unpack(ext, g * tall, breadth, cr[g])
        block1(g, carry)
        bcs[g] = pack(back, g * tall + SHIFT, breadth)
        column_back(g).start()

        @pl.when(i == 0)
        def _():
            brs[...] = back[height : height + SHIFT, 0:breadth, :].reshape(SHIFT * breadth, C).astype(BF16)
            bds[...] = (
                back[height : height + SHIFT, breadth : breadth + WIN, :].reshape(SHIFT * WIN, C).astype(BF16)
            )
            strips[2].start()
            strips[3].start()

        return carry

    lax.fori_loop(0, groups, step1, 0)

    def arrive(g):
        column_back(g).wait()
        unpack(back, g * tall + SHIFT, 0, bcr[g])

    def tail(i, carry):
        places = spots(i)
        z = jnp.concatenate(
            [
                (
                    first[pl.ds(r * WIN, WIN), pl.ds(0, 2 * WIN), :]
                    + back[pl.ds(r * WIN, WIN), pl.ds(0, 2 * WIN), :].astype(BF16).astype(F32)
                ).reshape(band, C)
                for r in places
            ],
            axis=0,
        )
        z = ffn(z, 1)
        for k, r in enumerate(places):
            out[pl.ds(r * WIN, WIN), pl.ds(0, 2 * WIN), :] = z[k * band : (k + 1) * band].reshape(
                WIN, 2 * WIN, C
            )
        return carry

    def store(g):
        rows = pl.ds(pl.multiple_of(g * tall, tall), tall)
        return pltpu.make_async_copy(out.at[rows], out_ref.at[rows], osem.at[g])

    def step2(i, carry):
        g = groups - 1 - i

        @pl.when(i == 0)
        def _():
            arrive(g)

        @pl.when(g > 0)
        def _():
            arrive(g - 1)

        @pl.when(g == 0)
        def _():
            strips[2].wait()
            strips[3].wait()
            back[0:SHIFT, 0:breadth, :] = brr[...].astype(F32).reshape(SHIFT, breadth, C)
            back[0:SHIFT, 0:SHIFT, :] = bdr[...].astype(F32).reshape(SHIFT, WIN, C)[:, :SHIFT]

        tail(g, carry)
        store(g).start()
        return carry

    lax.fori_loop(0, groups, step2, 0)
    for g in range(groups):
        store(g).wait()


def on_device(ny, nx, *operands):
    height, breadth, _ = operands[0].shape
    groups = height // (GROUP * WIN)
    col, row, corner = (groups, GROUP * WIN * SHIFT, C), (SHIFT * breadth, C), (SHIFT * WIN, C)
    hbm = pl.BlockSpec(memory_space=pltpu.HBM)
    return pl.pallas_call(
        functools.partial(kernel, ny, nx, height, breadth),
        out_shape=jax.ShapeDtypeStruct((height, breadth, C), F32),
        in_specs=[hbm] * len(operands),
        out_specs=hbm,
        scratch_shapes=[pltpu.VMEM(x.shape, x.dtype) for x in operands]
        + [
            pltpu.VMEM((height, breadth, C), F32),
            pltpu.VMEM((height, breadth, C), F32),
            pltpu.VMEM((height + SHIFT, breadth + WIN, C), F32),
            pltpu.VMEM((height + SHIFT, breadth + WIN, C), F32),
            pltpu.VMEM((3, HEADS * WIN * WIN, 2 * WIN * WIN), F32),
        ]
        + [pltpu.VMEM(shape, BF16) for shape in [col] * 4 + [row] * 4 + [corner] * 4]
        + [
            pltpu.SemaphoreType.DMA((2 * groups + 4,)),
            pltpu.SemaphoreType.DMA((2 * groups + 4,)),
            pltpu.SemaphoreType.DMA((len(operands),)),
            pltpu.SemaphoreType.DMA((groups,)),
        ],
        compiler_params=pltpu.CompilerParams(
            collective_id=0, has_side_effects=True, vmem_limit_bytes=48 * 1024 * 1024
        ),
        cost_estimate=pl.CostEstimate(flops=10**9, bytes_accessed=2 * 10**6, transcendentals=10**6),
    )(*operands)


def solution(mesh):
    return jax.shard_map(
        functools.partial(on_device, mesh.shape["gy"], mesh.shape["gx"]),
        mesh=mesh,
        in_specs=(P("gy", "gx", None), P(), P(), P(), P(), P(), P(), P()),
        out_specs=P("gy", "gx", None),
        check_vma=False,
    )
```

```python
import functools

import jax
import jax.numpy as jnp
from jax import lax
from jax.experimental import pallas as pl
from jax.experimental.pallas import tpu as pltpu
from jax.sharding import PartitionSpec as P

C = 128
HEADS = 4
WIN = 8
HD = 32
SHIFT = 4
EPSILON = 1e-05
F32 = jnp.float32
BF16 = jnp.bfloat16
GROUP = 2


def layer_norm(values, gain):
    center = values - jnp.mean(values, axis=-1, keepdims=True)
    spread = jnp.mean(center * center, axis=-1, keepdims=True)
    return center * lax.rsqrt(spread + EPSILON) * gain


ERFC = (0.254829592, -0.284496736, 1.421413741, -1.453152027, 1.061405429)
RATE = 0.3275911
POLE = 2**0.5 / RATE
TAIL = [0.5 * c * POLE ** (n + 1) for n, c in enumerate(ERFC)]


def gelu(x):
    a = jnp.abs(x)
    d = a + POLE
    t = pl.reciprocal(d, approx=True)
    t = t * (2.0 - d * t)
    poly = TAIL[4] * t + TAIL[3]
    for coef in TAIL[2::-1]:
        poly = poly * t + coef
    gauss = jnp.exp2((x * x) * (-0.5 * 1.4426950408889634))
    return jnp.maximum(x, 0.0) - (a * t) * (poly * gauss)


def window_pair(triple, bias, second, heads):
    triple = triple.reshape(WIN, 2 * WIN, 3 * C)
    query = triple[:, :, :C].reshape(2 * WIN * WIN, C)
    zero = jnp.zeros_like(query)
    query = jnp.concatenate(
        [jnp.where(second, zero, query), jnp.where(second, query, zero)], axis=1
    ).astype(BF16)
    keys, values = [], []
    for w in range(2):
        part = triple[:, w * WIN : (w + 1) * WIN, C:].reshape(WIN * WIN, 2 * C).astype(BF16)
        keys.append(jnp.concatenate([part[:, :C] * m for m in heads], axis=0))
        values.append(jnp.concatenate([part[:, C:] * m for m in heads], axis=0))
    keys = jnp.concatenate(keys, axis=1)
    values = jnp.concatenate(values, axis=1)
    scores = lax.dot_general(keys, query, (((1,), (1,)), ((), ())), preferred_element_type=F32)
    scores = (scores * HD ** (-0.5) + bias).reshape(HEADS, WIN * WIN, 2 * WIN * WIN)
    powers = jnp.exp(scores - jnp.max(scores, axis=1, keepdims=True))
    probs = powers * (1.0 / jnp.sum(powers, axis=1, keepdims=True))
    probs = probs.reshape(HEADS * WIN * WIN, 2 * WIN * WIN).astype(BF16)
    both = lax.dot_general(probs, values, (((0,), (0,)), ((), ())), preferred_element_type=F32)
    return jnp.where(second, both[:, C:], both[:, :C]).astype(BF16)


def kernel(
    ny, nx, height, breadth,
    feat_in, again_in, tw_in, ow_in, table_in, hgain_in, ew_in, sw_in, out_ref,
    feat, again, tw, ow, table, hgain, ew, sw, out,
    first, ext, back, bias, cs, cr, bcs, bcr, rs, rr, brs, brr, ds, dr, bds, bdr,
    ssem, rsem, isem, osem,
):
    loads = [
        pltpu.make_async_copy(src, dst, isem.at[k])
        for k, (src, dst) in enumerate(
            [
                (table_in, table), (feat_in, feat), (again_in, again), (tw_in, tw),
                (ow_in, ow), (hgain_in, hgain), (ew_in, ew), (sw_in, sw),
            ]
        )
    ]
    for load in loads:
        load.start()
    gy, gx = lax.axis_index("gy"), lax.axis_index("gx")
    up, down = lax.rem(gy + ny - 1, ny), lax.rem(gy + 1, ny)
    left, right = lax.rem(gx + nx - 1, nx), lax.rem(gx + 1, nx)
    barrier = pltpu.get_barrier_semaphore()
    around = [(up, gx), (gy, left), (up, left), (down, gx), (gy, right), (down, right)]
    for who in around:
        pl.semaphore_signal(barrier, inc=1, device_id=who, device_id_type=pl.DeviceIdType.MESH)

    jj = lax.broadcasted_iota(jnp.int32, (WIN, 2 * WIN * WIN), 0)
    lane = lax.broadcasted_iota(jnp.int32, (WIN, 2 * WIN * WIN), 1)
    col_cut = ((jj >= SHIFT) != (lane % WIN >= SHIFT)) & (lane % (2 * WIN) >= WIN) & (gx == nx - 1)
    extent = 2 * WIN - 1
    entry = lax.broadcasted_iota(jnp.int32, (extent * extent, 4 * WIN * WIN), 0)
    place = lax.broadcasted_iota(jnp.int32, (extent * extent, 4 * WIN * WIN), 1)
    pick = jnp.where(
        (entry == place // (2 * WIN) * extent + place % (2 * WIN)) & (place % (2 * WIN) < extent), 1.0, 0.0
    )
    first_half = lax.broadcasted_iota(jnp.int32, (WIN, 4 * WIN * WIN), 1) % (2 * WIN) < WIN
    loads[0].wait()
    spread_rows = [
        jnp.dot(table[b], pick, precision=lax.Precision.HIGHEST, preferred_element_type=F32) for b in range(2)
    ]
    for b in range(2):
        for h in range(HEADS):
            row = jnp.broadcast_to(spread_rows[b][h : h + 1], (WIN, 4 * WIN * WIN))
            rows = jnp.where(
                first_half,
                pltpu.roll(row, 4 * WIN * WIN - WIN + 1, 1, stride=1, stride_axis=0),
                pltpu.roll(row, 1, 1, stride=1, stride_axis=0),
            )
            for y in range(WIN):
                at = (WIN - 1 - y) * 2 * WIN
                piece = rows[:, at : at + 2 * WIN * WIN]
                spot = slice(h * 64 + y * WIN, h * 64 + (y + 1) * WIN)
                if b == 0:
                    bias[0, spot] = piece
                else:
                    row_cut = ((lane >= SHIFT * 2 * WIN) != (y >= SHIFT)) & (gy == ny - 1)
                    bias[1, spot] = piece + jnp.where(col_cut, -100.0, 0.0)
                    bias[2, spot] = piece + jnp.where(col_cut | row_cut, -100.0, 0.0)

    token = lax.broadcasted_iota(jnp.int32, (2 * WIN * WIN, C), 0)
    second = token % (2 * WIN) >= WIN
    channel = lax.broadcasted_iota(jnp.int32, (1, C), 1)
    heads = [jnp.where(channel // HD == h, 1.0, 0.0).astype(BF16) for h in range(HEADS)]
    bands = height // WIN
    band = 2 * WIN * WIN
    group = GROUP
    groups = bands // group
    tall = group * WIN

    def dot(a, b):
        return jnp.dot(a, b, preferred_element_type=F32)

    def spots(i):
        return [i * group + k for k in range(group)]

    def ffn(z, b):
        normed = layer_norm(z, hgain[b : b + 1]).astype(BF16)
        hidden = gelu(dot(normed, ew[b])).astype(BF16)
        return z + dot(hidden, sw[b])

    def block0(i, carry):
        places = spots(i)
        z = jnp.concatenate(
            [feat[pl.ds(r * WIN, WIN), pl.ds(0, 2 * WIN), :].reshape(band, C) for r in places], axis=0
        ).astype(F32)
        triple = dot(layer_norm(z, again[0:1]).astype(BF16), tw[0])
        ctx = [window_pair(triple[k * band : (k + 1) * band], bias[0], second, heads) for k in range(group)]
        branch = dot(jnp.concatenate(ctx, axis=0), ow[0]).astype(BF16).astype(F32)
        z = ffn(z + branch, 0)
        normed = layer_norm(z, again[1:2])
        for k, r in enumerate(places):
            spot = (pl.ds(r * WIN, WIN), pl.ds(0, 2 * WIN), slice(None))
            first[spot] = z[k * band : (k + 1) * band].reshape(WIN, 2 * WIN, C)
            ext[spot] = normed[k * band : (k + 1) * band].reshape(WIN, 2 * WIN, C)
        return carry

    def remote(src, dst, k, who):
        return pltpu.make_async_remote_copy(
            src_ref=src, dst_ref=dst, send_sem=ssem.at[k], recv_sem=rsem.at[k],
            device_id=who, device_id_type=pl.DeviceIdType.MESH,
        )

    def column(g):
        return remote(cs.at[g], cr.at[g], g, (gy, left))

    def column_back(g):
        return remote(bcs.at[g], bcr.at[g], groups + g, (gy, right))

    strips = [
        remote(rs, rr, 2 * groups, (up, gx)), remote(ds, dr, 2 * groups + 1, (up, left)),
        remote(brs, brr, 2 * groups + 2, (down, gx)), remote(bds, bdr, 2 * groups + 3, (down, right)),
    ]
    half = tall // 2

    def pack(ref, r0, c0):
        low = ref[pl.ds(r0, half), c0 : c0 + SHIFT, :]
        high = ref[pl.ds(r0 + half, half), c0 : c0 + SHIFT, :]
        return jnp.concatenate([low, high], axis=1).reshape(half * WIN, C).astype(BF16)

    def unpack(ref, r0, c0, buf):
        both = buf.astype(F32).reshape(half, WIN, C)
        ref[pl.ds(r0, half), c0 : c0 + SHIFT, :] = both[:, :SHIFT]
        ref[pl.ds(r0 + half, half), c0 : c0 + SHIFT, :] = both[:, SHIFT:]

    for load in loads[1:]:
        load.wait()

    def step0(i, carry):
        g = lax.rem(groups - i, groups)
        block0(g, carry)
        cs[g] = pack(ext, g * tall, 0)

        @pl.when(i == 0)
        def _():
            rs[...] = ext[0:SHIFT, 0:breadth, :].reshape(SHIFT * breadth, C).astype(BF16)
            ds[...] = ext[0:SHIFT, 0:WIN, :].reshape(SHIFT * WIN, C).astype(BF16)
            pl.semaphore_wait(barrier, 6)
            strips[0].start()
            strips[1].start()

        column(g).start()
        return carry

    lax.fori_loop(0, groups, step0, 0)

    def block1(i, carry):
        places = spots(i)
        x = jnp.concatenate(
            [
                ext[pl.ds(r * WIN + SHIFT, WIN), pl.ds(SHIFT, 2 * WIN), :].reshape(band, C)
                for r in places
            ],
            axis=0,
        ).astype(BF16)
        triple = dot(x, tw[1])
        ctx = [
            window_pair(
                triple[k * band : (k + 1) * band],
                bias[jnp.where(r == bands - 1, 2, 1)],
                second, heads,
            )
            for k, r in enumerate(places)
        ]
        branch = dot(jnp.concatenate(ctx, axis=0), ow[1])
        for k, r in enumerate(places):
            back[pl.ds(r * WIN + SHIFT, WIN), pl.ds(SHIFT, 2 * WIN), :] = branch[
                k * band : (k + 1) * band
            ].reshape(WIN, 2 * WIN, C)
        return carry

    def step1(i, carry):
        g = groups - 1 - i

        @pl.when(i == 0)
        def _():
            strips[0].wait()
            strips[1].wait()
            ext[height : height + SHIFT, 0:breadth, :] = rr[...].astype(F32).reshape(SHIFT, breadth, C)
            ext[height : height + SHIFT, breadth : breadth + SHIFT, :] = (
                dr[...].astype(F32).reshape(SHIFT, WIN, C)[:, :SHIFT]
            )

        column(g).wait()
        unpack(ext, g * tall, breadth, cr[g])
        block1(g, carry)
        bcs[g] = pack(back, g * tall + SHIFT, breadth)
        column_back(g).start()

        @pl.when(i == 0)
        def _():
            brs[...] = back[height : height + SHIFT, 0:breadth, :].reshape(SHIFT * breadth, C).astype(BF16)
            bds[...] = (
                back[height : height + SHIFT, breadth : breadth + WIN, :].reshape(SHIFT * WIN, C).astype(BF16)
            )
            strips[2].start()
            strips[3].start()

        return carry

    lax.fori_loop(0, groups, step1, 0)

    def arrive(g):
        column_back(g).wait()
        unpack(back, g * tall + SHIFT, 0, bcr[g])

    def tail(i, carry):
        places = spots(i)
        z = jnp.concatenate(
            [
                (
                    first[pl.ds(r * WIN, WIN), pl.ds(0, 2 * WIN), :]
                    + back[pl.ds(r * WIN, WIN), pl.ds(0, 2 * WIN), :].astype(BF16).astype(F32)
                ).reshape(band, C)
                for r in places
            ],
            axis=0,
        )
        z = ffn(z, 1)
        for k, r in enumerate(places):
            out[pl.ds(r * WIN, WIN), pl.ds(0, 2 * WIN), :] = z[k * band : (k + 1) * band].reshape(
                WIN, 2 * WIN, C
            )
        return carry

    def store(g):
        rows = pl.ds(pl.multiple_of(g * tall, tall), tall)
        return pltpu.make_async_copy(out.at[rows], out_ref.at[rows], osem.at[g])

    def step2(i, carry):
        g = groups - 1 - i

        @pl.when(i == 0)
        def _():
            arrive(g)

        @pl.when(g > 0)
        def _():
            arrive(g - 1)

        @pl.when(g == 0)
        def _():
            strips[2].wait()
            strips[3].wait()
            back[0:SHIFT, 0:breadth, :] = brr[...].astype(F32).reshape(SHIFT, breadth, C)
            back[0:SHIFT, 0:SHIFT, :] = bdr[...].astype(F32).reshape(SHIFT, WIN, C)[:, :SHIFT]

        tail(g, carry)
        store(g).start()
        return carry

    lax.fori_loop(0, groups, step2, 0)
    for g in range(groups):
        store(g).wait()


def on_device(ny, nx, *operands):
    height, breadth, _ = operands[0].shape
    groups = height // (GROUP * WIN)
    col, row, corner = (groups, GROUP * WIN * SHIFT, C), (SHIFT * breadth, C), (SHIFT * WIN, C)
    hbm = pl.BlockSpec(memory_space=pl.ANY)
    return pl.pallas_call(
        functools.partial(kernel, ny, nx, height, breadth),
        out_shape=jax.ShapeDtypeStruct((height, breadth, C), F32),
        in_specs=[hbm] * len(operands),
        out_specs=hbm,
        scratch_shapes=[pltpu.VMEM(x.shape, x.dtype) for x in operands]
        + [
            pltpu.VMEM((height, breadth, C), F32),
            pltpu.VMEM((height, breadth, C), F32),
            pltpu.VMEM((height + SHIFT, breadth + WIN, C), F32),
            pltpu.VMEM((height + SHIFT, breadth + WIN, C), F32),
            pltpu.VMEM((3, HEADS * WIN * WIN, 2 * WIN * WIN), F32),
        ]
        + [pltpu.VMEM(shape, BF16) for shape in [col] * 4 + [row] * 4 + [corner] * 4]
        + [
            pltpu.SemaphoreType.DMA((2 * groups + 4,)),
            pltpu.SemaphoreType.DMA((2 * groups + 4,)),
            pltpu.SemaphoreType.DMA((len(operands),)),
            pltpu.SemaphoreType.DMA((groups,)),
        ],
        compiler_params=pltpu.CompilerParams(
            collective_id=0, has_side_effects=True, vmem_limit_bytes=48 * 1024 * 1024
        ),
        cost_estimate=pl.CostEstimate(flops=10**9, bytes_accessed=2 * 10**6, transcendentals=10**6),
    )(*operands)


def solution(mesh):
    return jax.shard_map(
        functools.partial(on_device, mesh.shape["gy"], mesh.shape["gx"]),
        mesh=mesh,
        in_specs=(P("gy", "gx", None), P(), P(), P(), P(), P(), P(), P()),
        out_specs=P("gy", "gx", None),
        check_vma=False,
    )
```

```python
import functools

import jax
import jax.numpy as jnp
from jax import lax
from jax.experimental import pallas as pl
from jax.experimental.pallas import tpu as pltpu
from jax.sharding import PartitionSpec as P

C = 128
HEADS = 4
WIN = 8
HD = 32
SHIFT = 4
EPSILON = 1e-05
F32 = jnp.float32
BF16 = jnp.bfloat16
GROUP = 2


def layer_norm(values, gain):
    center = values - jnp.mean(values, axis=-1, keepdims=True)
    spread = jnp.mean(center * center, axis=-1, keepdims=True)
    return center * lax.rsqrt(spread + EPSILON) * gain


ERFC = (0.254829592, -0.284496736, 1.421413741, -1.453152027, 1.061405429)
RATE = 0.3275911
POLE = 2**0.5 / RATE
TAIL = [0.5 * c * POLE ** (n + 1) for n, c in enumerate(ERFC)]


def gelu(x):
    a = jnp.abs(x)
    d = a + POLE
    t = pl.reciprocal(d, approx=True)
    t = t * (2.0 - d * t)
    poly = TAIL[4] * t + TAIL[3]
    for coef in TAIL[2::-1]:
        poly = poly * t + coef
    gauss = jnp.exp2((x * x) * (-0.5 * 1.4426950408889634))
    return jnp.maximum(x, 0.0) - (a * t) * (poly * gauss)


def window_pair(triple, bias, second, heads):
    triple = triple.reshape(WIN, 2 * WIN, 3 * C)
    query = triple[:, :, :C].reshape(2 * WIN * WIN, C)
    zero = jnp.zeros_like(query)
    query = jnp.concatenate(
        [jnp.where(second, zero, query), jnp.where(second, query, zero)], axis=1
    ).astype(BF16)
    keys, values = [], []
    for w in range(2):
        part = triple[:, w * WIN : (w + 1) * WIN, C:].reshape(WIN * WIN, 2 * C).astype(BF16)
        keys.append(jnp.concatenate([part[:, :C] * m for m in heads], axis=0))
        values.append(jnp.concatenate([part[:, C:] * m for m in heads], axis=0))
    keys = jnp.concatenate(keys, axis=1)
    values = jnp.concatenate(values, axis=1)
    scores = lax.dot_general(keys, query, (((1,), (1,)), ((), ())), preferred_element_type=F32)
    scores = (scores * HD ** (-0.5) + bias).reshape(HEADS, WIN * WIN, 2 * WIN * WIN)
    powers = jnp.exp(scores - jnp.max(scores, axis=1, keepdims=True))
    probs = powers * (1.0 / jnp.sum(powers, axis=1, keepdims=True))
    probs = probs.reshape(HEADS * WIN * WIN, 2 * WIN * WIN).astype(BF16)
    both = lax.dot_general(probs, values, (((0,), (0,)), ((), ())), preferred_element_type=F32)
    return jnp.where(second, both[:, C:], both[:, :C]).astype(BF16)


def kernel(
    ny, nx, height, breadth,
    feat_in, again_in, tw_in, ow_in, table_in, hgain_in, ew_in, sw_in, out_ref,
    feat, again, tw, ow, table, hgain, ew, sw, out,
    first, ext, back, bias, cs, cr, bcs, bcr, rs, rr, brs, brr, ds, dr, bds, bdr,
    ssem, rsem, isem, osem,
):
    loads = [
        pltpu.make_async_copy(src, dst, isem.at[k])
        for k, (src, dst) in enumerate(
            [
                (table_in, table), (feat_in, feat), (again_in, again), (tw_in, tw),
                (ow_in, ow), (hgain_in, hgain), (ew_in, ew), (sw_in, sw),
            ]
        )
    ]
    for load in loads:
        load.start()
    gy, gx = lax.axis_index("gy"), lax.axis_index("gx")
    up, down = lax.rem(gy + ny - 1, ny), lax.rem(gy + 1, ny)
    left, right = lax.rem(gx + nx - 1, nx), lax.rem(gx + 1, nx)
    barrier = pltpu.get_barrier_semaphore()
    around = [(up, gx), (gy, left), (up, left), (down, gx), (gy, right), (down, right)]
    for who in around:
        pl.semaphore_signal(barrier, inc=1, device_id=who, device_id_type=pl.DeviceIdType.MESH)

    jj = lax.broadcasted_iota(jnp.int32, (WIN, 2 * WIN * WIN), 0)
    lane = lax.broadcasted_iota(jnp.int32, (WIN, 2 * WIN * WIN), 1)
    col_cut = ((jj >= SHIFT) != (lane & 7 >= SHIFT)) & (lane & 15 >= WIN) & (gx == nx - 1)
    extent = 2 * WIN - 1
    entry = lax.broadcasted_iota(jnp.int32, (extent * extent, 4 * WIN * WIN), 0)
    place = lax.broadcasted_iota(jnp.int32, (extent * extent, 4 * WIN * WIN), 1)
    pick = jnp.where(
        (entry == (place >> 4) * extent + (place & 15)) & ((place & 15) < extent), 1.0, 0.0
    )
    first_half = lax.broadcasted_iota(jnp.int32, (WIN, 4 * WIN * WIN), 1) & 15 < WIN
    loads[0].wait()
    spread_rows = [
        jnp.dot(table[b], pick, precision=lax.Precision.HIGHEST, preferred_element_type=F32) for b in range(2)
    ]
    for b in range(2):
        for h in range(HEADS):
            row = jnp.broadcast_to(spread_rows[b][h : h + 1], (WIN, 4 * WIN * WIN))
            rows = jnp.where(
                first_half,
                pltpu.roll(row, 4 * WIN * WIN - WIN + 1, 1, stride=1, stride_axis=0),
                pltpu.roll(row, 1, 1, stride=1, stride_axis=0),
            )
            for y in range(WIN):
                at = (WIN - 1 - y) * 2 * WIN
                piece = rows[:, at : at + 2 * WIN * WIN]
                spot = slice(h * 64 + y * WIN, h * 64 + (y + 1) * WIN)
                if b == 0:
                    bias[0, spot] = piece
                else:
                    row_cut = ((lane >= SHIFT * 2 * WIN) != (y >= SHIFT)) & (gy == ny - 1)
                    bias[1, spot] = piece + jnp.where(col_cut, -100.0, 0.0)
                    bias[2, spot] = piece + jnp.where(col_cut | row_cut, -100.0, 0.0)

    token = lax.broadcasted_iota(jnp.int32, (2 * WIN * WIN, C), 0)
    second = token & 15 >= WIN
    channel = lax.broadcasted_iota(jnp.int32, (1, C), 1)
    heads = [jnp.where(channel >> 5 == h, 1.0, 0.0).astype(BF16) for h in range(HEADS)]
    bands = height // WIN
    band = 2 * WIN * WIN
    group = GROUP
    groups = bands // group
    tall = group * WIN

    def dot(a, b):
        return jnp.dot(a, b, preferred_element_type=F32)

    wide = 2 * group

    def spots(first_band, count):
        return [lax.rem(first_band + k, bands) for k in range(count)]

    def ffn(z, b):
        normed = layer_norm(z, hgain[b : b + 1]).astype(BF16)
        hidden = gelu(dot(normed, ew[b])).astype(BF16)
        return z + dot(hidden, sw[b])

    def block0(i, carry):
        places = spots(i * wide, wide)
        z = jnp.concatenate(
            [feat[pl.ds(r * WIN, WIN), pl.ds(0, 2 * WIN), :].reshape(band, C) for r in places], axis=0
        ).astype(F32)
        triple = dot(layer_norm(z, again[0:1]).astype(BF16), tw[0])
        ctx = [window_pair(triple[k * band : (k + 1) * band], bias[0], second, heads) for k in range(wide)]
        branch = dot(jnp.concatenate(ctx, axis=0), ow[0]).astype(BF16).astype(F32)
        z = ffn(z + branch, 0)
        normed = layer_norm(z, again[1:2])
        for k, r in enumerate(places):
            spot = (pl.ds(r * WIN, WIN), pl.ds(0, 2 * WIN), slice(None))
            first[spot] = z[k * band : (k + 1) * band].reshape(WIN, 2 * WIN, C)
            ext[spot] = normed[k * band : (k + 1) * band].reshape(WIN, 2 * WIN, C)
        return carry

    def remote(src, dst, k, who):
        return pltpu.make_async_remote_copy(
            src_ref=src, dst_ref=dst, send_sem=ssem.at[k], recv_sem=rsem.at[k],
            device_id=who, device_id_type=pl.DeviceIdType.MESH,
        )

    def column(g):
        return remote(cs.at[g], cr.at[g], g, (gy, left))

    def column_back(g):
        return remote(bcs.at[g], bcr.at[g], groups + g, (gy, right))

    strips = [
        remote(rs, rr, 2 * groups, (up, gx)), remote(ds, dr, 2 * groups + 1, (up, left)),
        remote(brs, brr, 2 * groups + 2, (down, gx)), remote(bds, bdr, 2 * groups + 3, (down, right)),
    ]
    half = tall // 2

    def pack(ref, r0, c0):
        low = ref[pl.ds(r0, half), c0 : c0 + SHIFT, :]
        high = ref[pl.ds(r0 + half, half), c0 : c0 + SHIFT, :]
        return jnp.concatenate([low, high], axis=1).reshape(half * WIN, C).astype(BF16)

    def unpack(ref, r0, c0, buf):
        both = buf.astype(F32).reshape(half, WIN, C)
        ref[pl.ds(r0, half), c0 : c0 + SHIFT, :] = both[:, :SHIFT]
        ref[pl.ds(r0 + half, half), c0 : c0 + SHIFT, :] = both[:, SHIFT:]

    for load in loads[1:]:
        load.wait()

    def step0(i, carry):
        block0(i, carry)
        for k in range(2):
            cs[2 * i + k] = pack(ext, (2 * i + k) * tall, 0)

        @pl.when(i == 0)
        def _():
            rs[...] = ext[0:SHIFT, 0:breadth, :].reshape(SHIFT * breadth, C).astype(BF16)
            ds[...] = ext[0:SHIFT, 0:WIN, :].reshape(SHIFT * WIN, C).astype(BF16)
            pl.semaphore_wait(barrier, 6)
            strips[0].start()
            strips[1].start()

        for k in range(2):
            column(2 * i + k).start()
        return carry

    lax.fori_loop(0, groups // 2, step0, 0)

    def block1(i, carry):
        places = spots(i * group, group)
        x = jnp.concatenate(
            [
                ext[pl.ds(r * WIN + SHIFT, WIN), pl.ds(SHIFT, 2 * WIN), :].reshape(band, C)
                for r in places
            ],
            axis=0,
        ).astype(BF16)
        triple = dot(x, tw[1])
        ctx = [
            window_pair(
                triple[k * band : (k + 1) * band],
                bias[jnp.where(r == bands - 1, 2, 1)],
                second, heads,
            )
            for k, r in enumerate(places)
        ]
        branch = dot(jnp.concatenate(ctx, axis=0), ow[1])
        for k, r in enumerate(places):
            back[pl.ds(r * WIN + SHIFT, WIN), pl.ds(SHIFT, 2 * WIN), :] = branch[
                k * band : (k + 1) * band
            ].reshape(WIN, 2 * WIN, C)
        return carry

    def enter(g):
        column(g).wait()
        unpack(ext, g * tall, breadth, cr[g])

    def step1(g, carry):
        @pl.when(g == 0)
        def _():
            enter(g)

        @pl.when(g < groups - 1)
        def _():
            enter(g + 1)

        @pl.when(g == groups - 1)
        def _():
            strips[0].wait()
            strips[1].wait()
            ext[height : height + SHIFT, 0:breadth, :] = rr[...].astype(F32).reshape(SHIFT, breadth, C)
            ext[height : height + SHIFT, breadth : breadth + SHIFT, :] = (
                dr[...].astype(F32).reshape(SHIFT, WIN, C)[:, :SHIFT]
            )

        block1(g, carry)
        bcs[g] = pack(back, g * tall + SHIFT, breadth)
        column_back(g).start()

        @pl.when(g == groups - 1)
        def _():
            brs[...] = back[height : height + SHIFT, 0:breadth, :].reshape(SHIFT * breadth, C).astype(BF16)
            bds[...] = (
                back[height : height + SHIFT, breadth : breadth + WIN, :].reshape(SHIFT * WIN, C).astype(BF16)
            )
            strips[2].start()
            strips[3].start()

        return carry

    lax.fori_loop(0, groups, step1, 0)

    def arrive(g):
        column_back(g).wait()
        unpack(back, g * tall + SHIFT, 0, bcr[g])

    def tail(i, carry):
        places = spots(i * wide + group, wide)
        z = jnp.concatenate(
            [
                (
                    first[pl.ds(r * WIN, WIN), pl.ds(0, 2 * WIN), :]
                    + back[pl.ds(r * WIN, WIN), pl.ds(0, 2 * WIN), :].astype(BF16).astype(F32)
                ).reshape(band, C)
                for r in places
            ],
            axis=0,
        )
        z = ffn(z, 1)
        for k, r in enumerate(places):
            out[pl.ds(r * WIN, WIN), pl.ds(0, 2 * WIN), :] = z[k * band : (k + 1) * band].reshape(
                WIN, 2 * WIN, C
            )
        return carry

    def store(g):
        rows = pl.ds(pl.multiple_of(g * tall, tall), tall)
        return pltpu.make_async_copy(out.at[rows], out_ref.at[rows], osem.at[g])

    def step2(i, carry):
        @pl.when(i == 0)
        def _():
            arrive(0)

        arrive(2 * i + 1)

        @pl.when(i < groups // 2 - 1)
        def _():
            arrive(2 * i + 2)

        @pl.when(i == groups // 2 - 1)
        def _():
            strips[2].wait()
            strips[3].wait()
            back[0:SHIFT, 0:breadth, :] = brr[...].astype(F32).reshape(SHIFT, breadth, C)
            back[0:SHIFT, 0:SHIFT, :] = bdr[...].astype(F32).reshape(SHIFT, WIN, C)[:, :SHIFT]

        tail(i, carry)
        store(2 * i + 1).start()
        store(lax.rem(2 * i + 2, groups)).start()
        return carry

    lax.fori_loop(0, groups // 2, step2, 0)
    for g in range(groups):
        store(g).wait()


def on_device(ny, nx, *operands):
    height, breadth, _ = operands[0].shape
    groups = height // (GROUP * WIN)
    col, row, corner = (groups, GROUP * WIN * SHIFT, C), (SHIFT * breadth, C), (SHIFT * WIN, C)
    hbm = pl.BlockSpec(memory_space=pl.ANY)
    return pl.pallas_call(
        functools.partial(kernel, ny, nx, height, breadth),
        out_shape=jax.ShapeDtypeStruct((height, breadth, C), F32),
        in_specs=[hbm] * len(operands),
        out_specs=hbm,
        scratch_shapes=[pltpu.VMEM(x.shape, x.dtype) for x in operands]
        + [
            pltpu.VMEM((height, breadth, C), F32),
            pltpu.VMEM((height, breadth, C), F32),
            pltpu.VMEM((height + SHIFT, breadth + WIN, C), F32),
            pltpu.VMEM((height + SHIFT, breadth + WIN, C), F32),
            pltpu.VMEM((3, HEADS * WIN * WIN, 2 * WIN * WIN), F32),
        ]
        + [pltpu.VMEM(shape, BF16) for shape in [col] * 4 + [row] * 4 + [corner] * 4]
        + [
            pltpu.SemaphoreType.DMA((2 * groups + 4,)),
            pltpu.SemaphoreType.DMA((2 * groups + 4,)),
            pltpu.SemaphoreType.DMA((len(operands),)),
            pltpu.SemaphoreType.DMA((groups,)),
        ],
        compiler_params=pltpu.CompilerParams(
            collective_id=0, has_side_effects=True, vmem_limit_bytes=64 * 1024 * 1024
        ),
        cost_estimate=pl.CostEstimate(flops=10**9, bytes_accessed=2 * 10**6, transcendentals=10**6),
    )(*operands)


def solution(mesh):
    return jax.shard_map(
        functools.partial(on_device, mesh.shape["gy"], mesh.shape["gx"]),
        mesh=mesh,
        in_specs=(P("gy", "gx", None), P(), P(), P(), P(), P(), P(), P()),
        out_specs=P("gy", "gx", None),
        check_vma=False,
    )
```

```python
import functools

import jax
import jax.numpy as jnp
from jax import lax
from jax.experimental import pallas as pl
from jax.experimental.pallas import tpu as pltpu
from jax.sharding import PartitionSpec as P

C = 128
HEADS = 4
WIN = 8
HD = 32
SHIFT = 4
EPSILON = 1e-05
F32 = jnp.float32
BF16 = jnp.bfloat16
GROUP = 2


def lane_mean(x, share):
    high = x.astype(BF16)
    low = (x - high.astype(F32)).astype(BF16)
    return jnp.dot(jnp.concatenate([high, low], axis=1), share, preferred_element_type=F32)


def layer_norm(values, gain, share):
    center = values - lane_mean(values, share)
    spread = lane_mean(center * center, share)
    return center * lax.rsqrt(spread + EPSILON) * gain


ERFC = (0.254829592, -0.284496736, 1.421413741, -1.453152027, 1.061405429)
RATE = 0.3275911
POLE = 2**0.5 / RATE
TAIL = [0.5 * c * POLE ** (n + 1) for n, c in enumerate(ERFC)]


def gelu(x):
    a = jnp.abs(x)
    d = a + POLE
    t = pl.reciprocal(d, approx=True)
    t = t * (2.0 - d * t)
    poly = TAIL[4] * t + TAIL[3]
    for coef in TAIL[2::-1]:
        poly = poly * t + coef
    gauss = jnp.exp2((x * x) * (-0.5 * 1.4426950408889634))
    return jnp.maximum(x, 0.0) - (a * t) * (poly * gauss)


def window_pair(queries_keys, values, bias, second, lower, heads, head_rows):
    query = queries_keys[:, :C]
    zero = jnp.zeros_like(query)
    query = jnp.concatenate(
        [jnp.where(second, zero, query), jnp.where(second, query, zero)], axis=1
    ).astype(BF16)
    keys = []
    for w in range(2):
        part = queries_keys[w * WIN * WIN : (w + 1) * WIN * WIN, C:].astype(BF16)
        keys.append(jnp.concatenate([part * m for m in heads], axis=0))
    keys = jnp.concatenate(keys, axis=1)
    turned = pltpu.roll(values, WIN * WIN, 1)
    spread = [jnp.where(lower, values, turned).astype(BF16), jnp.where(lower, turned, values).astype(BF16)]
    spread = jnp.concatenate(
        [jnp.concatenate([part * m for m in head_rows], axis=1) for part in spread], axis=0
    )
    scores = lax.dot_general(keys, query, (((1,), (1,)), ((), ())), preferred_element_type=F32)
    scores = (scores * HD ** (-0.5) + bias).reshape(HEADS, WIN * WIN, 2 * WIN * WIN)
    powers = jnp.exp(scores - jnp.max(scores, axis=1, keepdims=True))
    probs = powers * (1.0 / jnp.sum(powers, axis=1, keepdims=True))
    probs = probs.reshape(HEADS * WIN * WIN, 2 * WIN * WIN).astype(BF16)
    both = jnp.dot(spread, probs, preferred_element_type=F32)
    return jnp.where(lower, both[:C], both[C:]).astype(BF16)


def kernel(
    ny, nx, height, breadth,
    feat_in, again_in, tw_in, ow_in, table_in, hgain_in, ew_in, sw_in, out_ref,
    feat, again, tw, ow, table, hgain, ew, sw, out,
    first, ext, back, bias, wide_rows, vt, cs, cr, bcs, bcr, rs, rr, brs, brr, ds, dr, bds, bdr,
    ssem, rsem, isem, osem,
):
    loads = [
        pltpu.make_async_copy(src, dst, isem.at[k])
        for k, (src, dst) in enumerate(
            [
                (table_in, table), (feat_in, feat), (again_in, again), (tw_in, tw),
                (ow_in, ow), (hgain_in, hgain), (ew_in, ew), (sw_in, sw),
            ]
        )
    ]
    for load in loads:
        load.start()
    gy, gx = lax.axis_index("gy"), lax.axis_index("gx")
    up, down = lax.rem(gy + ny - 1, ny), lax.rem(gy + 1, ny)
    left, right = lax.rem(gx + nx - 1, nx), lax.rem(gx + 1, nx)
    barrier = pltpu.get_barrier_semaphore()
    around = [(up, gx), (gy, left), (up, left), (down, gx), (gy, right), (down, right)]
    for who in around:
        pl.semaphore_signal(barrier, inc=1, device_id=who, device_id_type=pl.DeviceIdType.MESH)

    jj = lax.broadcasted_iota(jnp.int32, (WIN, 2 * WIN * WIN), 0)
    lane = lax.broadcasted_iota(jnp.int32, (WIN, 2 * WIN * WIN), 1)
    col_cut = ((jj >= SHIFT) != (lane & 7 >= SHIFT)) & (lane >= WIN * WIN) & (gx == nx - 1)
    extent = 2 * WIN - 1
    entry = lax.broadcasted_iota(jnp.int32, (extent * extent, 2 * WIN * WIN), 0)
    place = lax.broadcasted_iota(jnp.int32, (extent * extent, 2 * WIN * WIN), 1)
    target = entry - ((place >> 3) * extent + (place & 7) + WIN - 1)
    loads[0].wait()
    rest = jnp.concatenate([table[0], table[1]], axis=0)
    terms = []
    for _ in range(3):
        terms.append(rest.astype(BF16).astype(F32))
        rest = rest - terms[-1]
    terms = jnp.concatenate(terms, axis=0).astype(BF16)
    for x in range(WIN):
        pick = jnp.where(target == -x, 1.0, 0.0).astype(BF16)
        found = jnp.dot(terms, pick, preferred_element_type=F32)
        wide_rows[x] = found[:WIN] + found[WIN : 2 * WIN] + found[2 * WIN :]
    for b in range(2):
        for h in range(HEADS):
            rows = wide_rows[:, b * HEADS + h, :]
            for y in range(WIN):
                at = (WIN - 1 - y) * WIN
                piece = jnp.where(
                    lane < WIN * WIN,
                    pltpu.roll(rows, (2 * WIN * WIN - at) % (2 * WIN * WIN), 1),
                    pltpu.roll(rows, (WIN * WIN - at) % (2 * WIN * WIN), 1),
                )
                spot = slice(h * 64 + y * WIN, h * 64 + (y + 1) * WIN)
                if b == 0:
                    bias[0, spot] = piece
                else:
                    row_cut = ((lane & 63 >= SHIFT * WIN) != (y >= SHIFT)) & (gy == ny - 1)
                    bias[1, spot] = piece + jnp.where(col_cut, -100.0, 0.0)
                    bias[2, spot] = piece + jnp.where(col_cut | row_cut, -100.0, 0.0)

    token = lax.broadcasted_iota(jnp.int32, (2 * WIN * WIN, C), 0)
    second = token >= WIN * WIN
    lane_of = lax.broadcasted_iota(jnp.int32, (C, 2 * WIN * WIN), 1)
    row_of = lax.broadcasted_iota(jnp.int32, (C, 2 * WIN * WIN), 0)
    lower = lane_of < WIN * WIN
    head_rows = [
        jnp.where((row_of >> 5) == 2 * k + (lane_of >> 6), 1.0, 0.0).astype(BF16) for k in range(2)
    ]
    share = jnp.full((2 * C, C), 1.0 / C, BF16)
    channel = lax.broadcasted_iota(jnp.int32, (1, C), 1)
    heads = [jnp.where(channel >> 5 == h, 1.0, 0.0).astype(BF16) for h in range(HEADS)]
    bands = height // WIN
    band = 2 * WIN * WIN
    group = GROUP
    groups = bands // group
    tall = group * WIN

    def dot(a, b):
        return jnp.dot(a, b, preferred_element_type=F32)

    wide = 2 * group

    def spots(first_band, count):
        return [lax.rem(first_band + k, bands) for k in range(count)]

    def read(ref, r, c):
        return [ref[pl.ds(r, WIN), pl.ds(c + w * WIN, WIN), :].reshape(WIN * WIN, C) for w in range(2)]

    def write(ref, r, c, rows):
        for w in range(2):
            ref[pl.ds(r, WIN), pl.ds(c + w * WIN, WIN), :] = rows[
                w * WIN * WIN : (w + 1) * WIN * WIN
            ].reshape(WIN, WIN, C)

    def attend(x, b, biases):
        queries_keys = dot(x, tw[b, :, : 2 * C])
        branches = []
        for k, table_of in enumerate(biases):
            span = slice(k * band, (k + 1) * band)
            values = lax.dot_general(vt[b], x[span], (((1,), (1,)), ((), ())), preferred_element_type=F32)
            ctx = window_pair(
                queries_keys[span], values, bias[table_of], second, lower, heads, head_rows
            )
            branches.append(
                lax.dot_general(ctx, ow[b], (((0,), (0,)), ((), ())), preferred_element_type=F32)
            )
        return jnp.concatenate(branches, axis=0)

    def ffn(z, b):
        normed = layer_norm(z, hgain[b : b + 1], share).astype(BF16)
        hidden = gelu(dot(normed, ew[b])).astype(BF16)
        return z + dot(hidden, sw[b])

    def block0(i, carry):
        places = spots(i * wide, wide)
        z = jnp.concatenate([part for r in places for part in read(feat, r * WIN, 0)], axis=0).astype(F32)
        branch = attend(layer_norm(z, again[0:1], share).astype(BF16), 0, [0] * wide)
        z = ffn(z + branch.astype(BF16).astype(F32), 0)
        normed = layer_norm(z, again[1:2], share)
        for k, r in enumerate(places):
            write(first, r * WIN, 0, z[k * band : (k + 1) * band])
            write(ext, r * WIN, 0, normed[k * band : (k + 1) * band])
        return carry

    def remote(src, dst, k, who):
        return pltpu.make_async_remote_copy(
            src_ref=src, dst_ref=dst, send_sem=ssem.at[k], recv_sem=rsem.at[k],
            device_id=who, device_id_type=pl.DeviceIdType.MESH,
        )

    def column(g):
        return remote(cs.at[g], cr.at[g], g, (gy, left))

    def column_back(g):
        return remote(bcs.at[g], bcr.at[g], groups + g, (gy, right))

    strips = [
        remote(rs, rr, 2 * groups, (up, gx)), remote(ds, dr, 2 * groups + 1, (up, left)),
        remote(brs, brr, 2 * groups + 2, (down, gx)), remote(bds, bdr, 2 * groups + 3, (down, right)),
    ]
    half = tall // 2

    def pack(ref, r0, c0):
        low = ref[pl.ds(r0, half), c0 : c0 + SHIFT, :]
        high = ref[pl.ds(r0 + half, half), c0 : c0 + SHIFT, :]
        return jnp.concatenate([low, high], axis=1).reshape(half * WIN, C).astype(BF16)

    def unpack(ref, r0, c0, buf):
        both = buf.astype(F32).reshape(half, WIN, C)
        ref[pl.ds(r0, half), c0 : c0 + SHIFT, :] = both[:, :SHIFT]
        ref[pl.ds(r0 + half, half), c0 : c0 + SHIFT, :] = both[:, SHIFT:]

    for load in loads[1:]:
        load.wait()
    for b in range(2):
        vt[b] = tw[b, :, 2 * C :].astype(F32).T.astype(BF16)

    def step0(i, carry):
        block0(i, carry)
        for k in range(2):
            cs[2 * i + k] = pack(ext, (2 * i + k) * tall, 0)

        @pl.when(i == 0)
        def _():
            rs[...] = ext[0:SHIFT, 0:breadth, :].reshape(SHIFT * breadth, C).astype(BF16)
            ds[...] = ext[0:SHIFT, 0:WIN, :].reshape(SHIFT * WIN, C).astype(BF16)
            pl.semaphore_wait(barrier, 6)
            strips[0].start()
            strips[1].start()

        for k in range(2):
            column(2 * i + k).start()
        return carry

    lax.fori_loop(0, groups // 2, step0, 0)

    def block1(i, carry):
        places = spots(i * group, group)
        x = jnp.concatenate([part for r in places for part in read(ext, r * WIN + SHIFT, SHIFT)], axis=0)
        branch = attend(x.astype(BF16), 1, [jnp.where(r == bands - 1, 2, 1) for r in places])
        for k, r in enumerate(places):
            write(back, r * WIN + SHIFT, SHIFT, branch[k * band : (k + 1) * band])
        return carry

    def enter(g):
        column(g).wait()
        unpack(ext, g * tall, breadth, cr[g])

    def step1(g, carry):
        @pl.when(g == 0)
        def _():
            enter(g)

        @pl.when(g < groups - 1)
        def _():
            enter(g + 1)

        @pl.when(g == groups - 1)
        def _():
            strips[0].wait()
            strips[1].wait()
            ext[height : height + SHIFT, 0:breadth, :] = rr[...].astype(F32).reshape(SHIFT, breadth, C)
            ext[height : height + SHIFT, breadth : breadth + SHIFT, :] = (
                dr[...].astype(F32).reshape(SHIFT, WIN, C)[:, :SHIFT]
            )

        block1(g, carry)
        bcs[g] = pack(back, g * tall + SHIFT, breadth)
        column_back(g).start()

        @pl.when(g == groups - 1)
        def _():
            brs[...] = back[height : height + SHIFT, 0:breadth, :].reshape(SHIFT * breadth, C).astype(BF16)
            bds[...] = (
                back[height : height + SHIFT, breadth : breadth + WIN, :].reshape(SHIFT * WIN, C).astype(BF16)
            )
            strips[2].start()
            strips[3].start()

        return carry

    lax.fori_loop(0, groups, step1, 0)

    def arrive(g):
        column_back(g).wait()
        unpack(back, g * tall + SHIFT, 0, bcr[g])

    def tail(i, carry):
        places = spots(i * wide + group, wide)
        z = jnp.concatenate(
            [
                (
                    first[pl.ds(r * WIN, WIN), pl.ds(0, 2 * WIN), :]
                    + back[pl.ds(r * WIN, WIN), pl.ds(0, 2 * WIN), :].astype(BF16).astype(F32)
                ).reshape(band, C)
                for r in places
            ],
            axis=0,
        )
        z = ffn(z, 1)
        for k, r in enumerate(places):
            out[pl.ds(r * WIN, WIN), pl.ds(0, 2 * WIN), :] = z[k * band : (k + 1) * band].reshape(
                WIN, 2 * WIN, C
            )
        return carry

    def store(g):
        rows = pl.ds(pl.multiple_of(g * tall, tall), tall)
        return pltpu.make_async_copy(out.at[rows], out_ref.at[rows], osem.at[g])

    def step2(i, carry):
        @pl.when(i == 0)
        def _():
            arrive(0)

        arrive(2 * i + 1)

        @pl.when(i < groups // 2 - 1)
        def _():
            arrive(2 * i + 2)

        @pl.when(i == groups // 2 - 1)
        def _():
            strips[2].wait()
            strips[3].wait()
            back[0:SHIFT, 0:breadth, :] = brr[...].astype(F32).reshape(SHIFT, breadth, C)
            back[0:SHIFT, 0:SHIFT, :] = bdr[...].astype(F32).reshape(SHIFT, WIN, C)[:, :SHIFT]

        tail(i, carry)
        store(2 * i + 1).start()
        store(lax.rem(2 * i + 2, groups)).start()
        return carry

    lax.fori_loop(0, groups // 2, step2, 0)
    for g in range(groups):
        store(g).wait()


def on_device(ny, nx, *operands):
    height, breadth, _ = operands[0].shape
    groups = height // (GROUP * WIN)
    col, row, corner = (groups, GROUP * WIN * SHIFT, C), (SHIFT * breadth, C), (SHIFT * WIN, C)
    hbm = pl.BlockSpec(memory_space=pl.ANY)
    return pl.pallas_call(
        functools.partial(kernel, ny, nx, height, breadth),
        out_shape=jax.ShapeDtypeStruct((height, breadth, C), F32),
        in_specs=[hbm] * len(operands),
        out_specs=hbm,
        scratch_shapes=[pltpu.VMEM(x.shape, x.dtype) for x in operands]
        + [
            pltpu.VMEM((height, breadth, C), F32),
            pltpu.VMEM((height, breadth, C), F32),
            pltpu.VMEM((height + SHIFT, breadth + WIN, C), F32),
            pltpu.VMEM((height + SHIFT, breadth + WIN, C), F32),
            pltpu.VMEM((3, HEADS * WIN * WIN, 2 * WIN * WIN), F32),
            pltpu.VMEM((WIN, 2 * HEADS, 2 * WIN * WIN), F32),
            pltpu.VMEM((2, C, C), BF16),
        ]
        + [pltpu.VMEM(shape, BF16) for shape in [col] * 4 + [row] * 4 + [corner] * 4]
        + [
            pltpu.SemaphoreType.DMA((2 * groups + 4,)),
            pltpu.SemaphoreType.DMA((2 * groups + 4,)),
            pltpu.SemaphoreType.DMA((len(operands),)),
            pltpu.SemaphoreType.DMA((groups,)),
        ],
        compiler_params=pltpu.CompilerParams(
            collective_id=0, has_side_effects=True, vmem_limit_bytes=64 * 1024 * 1024
        ),
        cost_estimate=pl.CostEstimate(flops=10**9, bytes_accessed=2 * 10**6, transcendentals=10**6),
    )(*operands)


def solution(mesh):
    return jax.shard_map(
        functools.partial(on_device, mesh.shape["gy"], mesh.shape["gx"]),
        mesh=mesh,
        in_specs=(P("gy", "gx", None), P(), P(), P(), P(), P(), P(), P()),
        out_specs=P("gy", "gx", None),
        check_vma=False,
    )
```

```python
import functools

import jax
import jax.numpy as jnp
from jax import lax
from jax.experimental import pallas as pl
from jax.experimental.pallas import tpu as pltpu
from jax.sharding import PartitionSpec as P

C = 128
HEADS = 4
WIN = 8
HD = 32
SHIFT = 4
EPSILON = 1e-05
F32 = jnp.float32
BF16 = jnp.bfloat16
GROUP = 2


def layer_norm(values, gain):
    center = values - jnp.mean(values, axis=-1, keepdims=True)
    spread = jnp.mean(center * center, axis=-1, keepdims=True)
    return center * lax.rsqrt(spread + EPSILON) * gain


ERFC = (0.254829592, -0.284496736, 1.421413741, -1.453152027, 1.061405429)
RATE = 0.3275911
POLE = 2**0.5 / RATE
TAIL = [0.5 * c * POLE ** (n + 1) for n, c in enumerate(ERFC)]


def gelu(x):
    a = jnp.abs(x)
    d = a + POLE
    t = pl.reciprocal(d, approx=True)
    t = t * (2.0 - d * t)
    poly = TAIL[4] * t + TAIL[3]
    for coef in TAIL[2::-1]:
        poly = poly * t + coef
    gauss = jnp.exp2((x * x) * (-0.5 * 1.4426950408889634))
    return jnp.maximum(x, 0.0) - (a * t) * (poly * gauss)


def window_pair(triple, bias, second, heads):
    triple = triple.reshape(WIN, 2 * WIN, 3 * C)
    query = triple[:, :, :C].reshape(2 * WIN * WIN, C)
    zero = jnp.zeros_like(query)
    query = jnp.concatenate(
        [jnp.where(second, zero, query), jnp.where(second, query, zero)], axis=1
    ).astype(BF16)
    keys, values = [], []
    for w in range(2):
        part = triple[:, w * WIN : (w + 1) * WIN, C:].reshape(WIN * WIN, 2 * C).astype(BF16)
        keys.append(jnp.concatenate([part[:, :C] * m for m in heads], axis=0))
        values.append(jnp.concatenate([part[:, C:] * m for m in heads], axis=0))
    keys = jnp.concatenate(keys, axis=1)
    values = jnp.concatenate(values, axis=1)
    scores = lax.dot_general(keys, query, (((1,), (1,)), ((), ())), preferred_element_type=F32)
    scores = (scores * HD ** (-0.5) + bias).reshape(HEADS, WIN * WIN, 2 * WIN * WIN)
    powers = jnp.exp(scores - jnp.max(scores, axis=1, keepdims=True))
    probs = powers * (1.0 / jnp.sum(powers, axis=1, keepdims=True))
    probs = probs.reshape(HEADS * WIN * WIN, 2 * WIN * WIN).astype(BF16)
    both = lax.dot_general(probs, values, (((0,), (0,)), ((), ())), preferred_element_type=F32)
    return jnp.where(second, both[:, C:], both[:, :C]).astype(BF16)


def kernel(
    ny, nx, height, breadth,
    feat_in, again_in, tw_in, ow_in, table_in, hgain_in, ew_in, sw_in, out_ref,
    feat, again, tw, ow, table, hgain, ew, sw, out,
    first, ext, back, bias, cs, cr, bcs, bcr, rs, rr, brs, brr, ds, dr, bds, bdr,
    ssem, rsem, isem, osem,
):
    loads = [
        pltpu.make_async_copy(src, dst, isem.at[k])
        for k, (src, dst) in enumerate(
            [
                (table_in, table), (feat_in, feat), (again_in, again), (tw_in, tw),
                (ow_in, ow), (hgain_in, hgain), (ew_in, ew), (sw_in, sw),
            ]
        )
    ]
    for load in loads:
        load.start()
    gy, gx = lax.axis_index("gy"), lax.axis_index("gx")
    up, down = lax.rem(gy + ny - 1, ny), lax.rem(gy + 1, ny)
    left, right = lax.rem(gx + nx - 1, nx), lax.rem(gx + 1, nx)
    barrier = pltpu.get_barrier_semaphore()
    around = [(up, gx), (gy, left), (up, left), (down, gx), (gy, right), (down, right)]
    for who in around:
        pl.semaphore_signal(barrier, inc=1, device_id=who, device_id_type=pl.DeviceIdType.MESH)

    jj = lax.broadcasted_iota(jnp.int32, (WIN, 2 * WIN * WIN), 0)
    lane = lax.broadcasted_iota(jnp.int32, (WIN, 2 * WIN * WIN), 1)
    col_cut = ((jj >= SHIFT) != (lane & 7 >= SHIFT)) & (lane & 15 >= WIN) & (gx == nx - 1)
    extent = 2 * WIN - 1
    entry = lax.broadcasted_iota(jnp.int32, (extent * extent, 4 * WIN * WIN), 0)
    place = lax.broadcasted_iota(jnp.int32, (extent * extent, 4 * WIN * WIN), 1)
    pick = jnp.where(
        (entry == (place >> 4) * extent + (place & 15)) & ((place & 15) < extent), 1.0, 0.0
    )
    first_half = lax.broadcasted_iota(jnp.int32, (WIN, 4 * WIN * WIN), 1) & 15 < WIN
    loads[0].wait()
    spread_rows = [
        jnp.dot(table[b], pick, precision=lax.Precision.HIGHEST, preferred_element_type=F32) for b in range(2)
    ]
    for b in range(2):
        for h in range(HEADS):
            row = jnp.broadcast_to(spread_rows[b][h : h + 1], (WIN, 4 * WIN * WIN))
            rows = jnp.where(
                first_half,
                pltpu.roll(row, 4 * WIN * WIN - WIN + 1, 1, stride=1, stride_axis=0),
                pltpu.roll(row, 1, 1, stride=1, stride_axis=0),
            )
            for y in range(WIN):
                at = (WIN - 1 - y) * 2 * WIN
                piece = rows[:, at : at + 2 * WIN * WIN]
                spot = slice(h * 64 + y * WIN, h * 64 + (y + 1) * WIN)
                if b == 0:
                    bias[0, spot] = piece
                else:
                    row_cut = ((lane >= SHIFT * 2 * WIN) != (y >= SHIFT)) & (gy == ny - 1)
                    bias[1, spot] = piece + jnp.where(col_cut, -100.0, 0.0)
                    bias[2, spot] = piece + jnp.where(col_cut | row_cut, -100.0, 0.0)

    token = lax.broadcasted_iota(jnp.int32, (2 * WIN * WIN, C), 0)
    second = token & 15 >= WIN
    channel = lax.broadcasted_iota(jnp.int32, (1, C), 1)
    heads = [jnp.where(channel >> 5 == h, 1.0, 0.0).astype(BF16) for h in range(HEADS)]
    bands = height // WIN
    band = 2 * WIN * WIN
    group = GROUP
    groups = bands // group
    tall = group * WIN

    def dot(a, b):
        return jnp.dot(a, b, preferred_element_type=F32)

    wide = 2 * group

    def spots(first_band, count):
        return [lax.rem(first_band + k, bands) for k in range(count)]

    def ffn(z, b):
        normed = layer_norm(z, hgain[b : b + 1]).astype(BF16)
        hidden = gelu(dot(normed, ew[b])).astype(BF16)
        return z + dot(hidden, sw[b])

    def block0(i, carry):
        places = spots(i * wide, wide)
        z = jnp.concatenate(
            [feat[pl.ds(r * WIN, WIN), pl.ds(0, 2 * WIN), :].reshape(band, C) for r in places], axis=0
        ).astype(F32)
        triple = dot(layer_norm(z, again[0:1]).astype(BF16), tw[0])
        ctx = [window_pair(triple[k * band : (k + 1) * band], bias[0], second, heads) for k in range(wide)]
        branch = dot(jnp.concatenate(ctx, axis=0), ow[0]).astype(BF16).astype(F32)
        z = ffn(z + branch, 0)
        normed = layer_norm(z, again[1:2])
        for k, r in enumerate(places):
            spot = (pl.ds(r * WIN, WIN), pl.ds(0, 2 * WIN), slice(None))
            first[spot] = z[k * band : (k + 1) * band].reshape(WIN, 2 * WIN, C)
            ext[spot] = normed[k * band : (k + 1) * band].reshape(WIN, 2 * WIN, C)
        return carry

    def remote(src, dst, k, who):
        return pltpu.make_async_remote_copy(
            src_ref=src, dst_ref=dst, send_sem=ssem.at[k], recv_sem=rsem.at[k],
            device_id=who, device_id_type=pl.DeviceIdType.MESH,
        )

    def column(g):
        return remote(cs.at[g], cr.at[g], g, (gy, left))

    def column_back(g):
        return remote(bcs.at[g], bcr.at[g], groups + g, (gy, right))

    strips = [
        remote(rs, rr, 2 * groups, (up, gx)), remote(ds, dr, 2 * groups + 1, (up, left)),
        remote(brs, brr, 2 * groups + 2, (down, gx)), remote(bds, bdr, 2 * groups + 3, (down, right)),
    ]
    half = tall // 2

    def pack(ref, r0, c0):
        low = ref[pl.ds(r0, half), c0 : c0 + SHIFT, :]
        high = ref[pl.ds(r0 + half, half), c0 : c0 + SHIFT, :]
        return jnp.concatenate([low, high], axis=1).reshape(half * WIN, C).astype(BF16)

    def unpack(ref, r0, c0, buf):
        both = buf.astype(F32).reshape(half, WIN, C)
        ref[pl.ds(r0, half), c0 : c0 + SHIFT, :] = both[:, :SHIFT]
        ref[pl.ds(r0 + half, half), c0 : c0 + SHIFT, :] = both[:, SHIFT:]

    for load in loads[1:]:
        load.wait()

    def step0(i, carry):
        block0(i, carry)
        for k in range(2):
            cs[2 * i + k] = pack(ext, (2 * i + k) * tall, 0)

        @pl.when(i == 0)
        def _():
            rs[...] = ext[0:SHIFT, 0:breadth, :].reshape(SHIFT * breadth, C).astype(BF16)
            ds[...] = ext[0:SHIFT, 0:WIN, :].reshape(SHIFT * WIN, C).astype(BF16)
            pl.semaphore_wait(barrier, 6)
            strips[0].start()
            strips[1].start()

        for k in range(2):
            column(2 * i + k).start()
        return carry

    lax.fori_loop(0, groups // 2, step0, 0)

    def block1(i, carry):
        places = spots(i * group, group)
        x = jnp.concatenate(
            [
                ext[pl.ds(r * WIN + SHIFT, WIN), pl.ds(SHIFT, 2 * WIN), :].reshape(band, C)
                for r in places
            ],
            axis=0,
        ).astype(BF16)
        triple = dot(x, tw[1])
        ctx = [
            window_pair(
                triple[k * band : (k + 1) * band],
                bias[jnp.where(r == bands - 1, 2, 1)],
                second, heads,
            )
            for k, r in enumerate(places)
        ]
        branch = dot(jnp.concatenate(ctx, axis=0), ow[1])
        for k, r in enumerate(places):
            back[pl.ds(r * WIN + SHIFT, WIN), pl.ds(SHIFT, 2 * WIN), :] = branch[
                k * band : (k + 1) * band
            ].reshape(WIN, 2 * WIN, C)
        return carry

    def enter(g):
        column(g).wait()
        unpack(ext, g * tall, breadth, cr[g])

    def step1(g, carry):
        @pl.when(g == 0)
        def _():
            enter(g)

        @pl.when(g < groups - 1)
        def _():
            enter(g + 1)

        @pl.when(g == groups - 1)
        def _():
            strips[0].wait()
            strips[1].wait()
            ext[height : height + SHIFT, 0:breadth, :] = rr[...].astype(F32).reshape(SHIFT, breadth, C)
            ext[height : height + SHIFT, breadth : breadth + SHIFT, :] = (
                dr[...].astype(F32).reshape(SHIFT, WIN, C)[:, :SHIFT]
            )

        block1(g, carry)
        bcs[g] = pack(back, g * tall + SHIFT, breadth)
        column_back(g).start()

        @pl.when(g == groups - 1)
        def _():
            brs[...] = back[height : height + SHIFT, 0:breadth, :].reshape(SHIFT * breadth, C).astype(BF16)
            bds[...] = (
                back[height : height + SHIFT, breadth : breadth + WIN, :].reshape(SHIFT * WIN, C).astype(BF16)
            )
            strips[2].start()
            strips[3].start()

        return carry

    lax.fori_loop(0, groups, step1, 0)

    def arrive(g):
        column_back(g).wait()
        unpack(back, g * tall + SHIFT, 0, bcr[g])

    def tail(i, carry):
        places = spots(i * wide + group, wide)
        z = jnp.concatenate(
            [
                (
                    first[pl.ds(r * WIN, WIN), pl.ds(0, 2 * WIN), :]
                    + back[pl.ds(r * WIN, WIN), pl.ds(0, 2 * WIN), :].astype(BF16).astype(F32)
                ).reshape(band, C)
                for r in places
            ],
            axis=0,
        )
        for k, r in enumerate(places):
            out[pl.ds(r * WIN, WIN), pl.ds(0, 2 * WIN), :] = z[k * band : (k + 1) * band].reshape(
                WIN, 2 * WIN, C
            )
        return carry

    def store(g):
        rows = pl.ds(pl.multiple_of(g * tall, tall), tall)
        return pltpu.make_async_copy(out.at[rows], out_ref.at[rows], osem.at[g])

    def step2(i, carry):
        @pl.when(i == 0)
        def _():
            arrive(0)

        arrive(2 * i + 1)

        @pl.when(i < groups // 2 - 1)
        def _():
            arrive(2 * i + 2)

        @pl.when(i == groups // 2 - 1)
        def _():
            strips[2].wait()
            strips[3].wait()
            back[0:SHIFT, 0:breadth, :] = brr[...].astype(F32).reshape(SHIFT, breadth, C)
            back[0:SHIFT, 0:SHIFT, :] = bdr[...].astype(F32).reshape(SHIFT, WIN, C)[:, :SHIFT]

        tail(i, carry)
        store(2 * i + 1).start()
        store(lax.rem(2 * i + 2, groups)).start()
        return carry

    lax.fori_loop(0, groups // 2, step2, 0)
    for g in range(groups):
        store(g).wait()


def finish(z_ref, gain, ew, sw, out):
    shape = z_ref.shape
    z = z_ref[...].reshape(-1, C)
    normed = layer_norm(z, gain[1:2]).astype(BF16)
    hidden = gelu(jnp.dot(normed, ew[0], preferred_element_type=F32)).astype(BF16)
    out[...] = (z + jnp.dot(hidden, sw[0], preferred_element_type=F32)).reshape(shape)


def on_device(ny, nx, *operands):
    height, breadth, _ = operands[0].shape
    groups = height // (GROUP * WIN)
    col, row, corner = (groups, GROUP * WIN * SHIFT, C), (SHIFT * breadth, C), (SHIFT * WIN, C)
    hbm = pl.BlockSpec(memory_space=pl.ANY)
    middle = pl.pallas_call(
        functools.partial(kernel, ny, nx, height, breadth),
        out_shape=jax.ShapeDtypeStruct((height, breadth, C), F32),
        in_specs=[hbm] * len(operands),
        out_specs=hbm,
        scratch_shapes=[pltpu.VMEM(x.shape, x.dtype) for x in operands]
        + [
            pltpu.VMEM((height, breadth, C), F32),
            pltpu.VMEM((height, breadth, C), F32),
            pltpu.VMEM((height + SHIFT, breadth + WIN, C), F32),
            pltpu.VMEM((height + SHIFT, breadth + WIN, C), F32),
            pltpu.VMEM((3, HEADS * WIN * WIN, 2 * WIN * WIN), F32),
        ]
        + [pltpu.VMEM(shape, BF16) for shape in [col] * 4 + [row] * 4 + [corner] * 4]
        + [
            pltpu.SemaphoreType.DMA((2 * groups + 4,)),
            pltpu.SemaphoreType.DMA((2 * groups + 4,)),
            pltpu.SemaphoreType.DMA((len(operands),)),
            pltpu.SemaphoreType.DMA((groups,)),
        ],
        compiler_params=pltpu.CompilerParams(
            collective_id=0, has_side_effects=True, vmem_limit_bytes=64 * 1024 * 1024
        ),
        cost_estimate=pl.CostEstimate(flops=10**9, bytes_accessed=2 * 10**6, transcendentals=10**6),
    )(*operands)
    hidden_gain, expand_weight, shrink_weight = operands[5:]
    tile = pl.BlockSpec((2 * GROUP * WIN, breadth, C), lambda i: (i, 0, 0))
    return pl.pallas_call(
        finish,
        grid=(height // (2 * GROUP * WIN),),
        out_shape=jax.ShapeDtypeStruct((height, breadth, C), F32),
        in_specs=[
            tile,
            pl.BlockSpec(hidden_gain.shape, lambda i: (0, 0)),
            pl.BlockSpec((1, *expand_weight.shape[1:]), lambda i: (1, 0, 0)),
            pl.BlockSpec((1, *shrink_weight.shape[1:]), lambda i: (1, 0, 0)),
        ],
        out_specs=tile,
        compiler_params=pltpu.CompilerParams(vmem_limit_bytes=64 * 1024 * 1024),
    )(middle, hidden_gain, expand_weight, shrink_weight)


def solution(mesh):
    return jax.shard_map(
        functools.partial(on_device, mesh.shape["gy"], mesh.shape["gx"]),
        mesh=mesh,
        in_specs=(P("gy", "gx", None), P(), P(), P(), P(), P(), P(), P()),
        out_specs=P("gy", "gx", None),
        check_vma=False,
    )
```

```python
import functools

import jax
import jax.numpy as jnp
from jax import lax
from jax.experimental import pallas as pl
from jax.experimental.pallas import tpu as pltpu
from jax.sharding import PartitionSpec as P

C = 128
HEADS = 4
WIN = 8
HD = 32
SHIFT = 4
EPSILON = 1e-05
F32 = jnp.float32
BF16 = jnp.bfloat16
GROUP = 2


def layer_norm(values, gain):
    center = values - jnp.mean(values, axis=-1, keepdims=True)
    spread = jnp.mean(center * center, axis=-1, keepdims=True)
    return center * lax.rsqrt(spread + EPSILON) * gain


ERFC = (0.254829592, -0.284496736, 1.421413741, -1.453152027, 1.061405429)
RATE = 0.3275911
POLE = 2**0.5 / RATE
TAIL = [0.5 * c * POLE ** (n + 1) for n, c in enumerate(ERFC)]


def gelu(x):
    a = jnp.abs(x)
    d = a + POLE
    t = pl.reciprocal(d, approx=True)
    t = t * (2.0 - d * t)
    poly = TAIL[4] * t + TAIL[3]
    for coef in TAIL[2::-1]:
        poly = poly * t + coef
    gauss = jnp.exp2((x * x) * (-0.5 * 1.4426950408889634))
    return jnp.maximum(x, 0.0) - (a * t) * (poly * gauss)


def window_pair(queries_keys, values, bias, second, lower, heads, head_rows):
    query = queries_keys[:, :C]
    zero = jnp.zeros_like(query)
    query = jnp.concatenate(
        [jnp.where(second, zero, query), jnp.where(second, query, zero)], axis=1
    ).astype(BF16)
    keys = []
    for w in range(2):
        part = queries_keys[w * WIN * WIN : (w + 1) * WIN * WIN, C:].astype(BF16)
        keys.append(jnp.concatenate([part * m for m in heads], axis=0))
    keys = jnp.concatenate(keys, axis=1)
    turned = pltpu.roll(values, WIN * WIN, 1)
    spread = [jnp.where(lower, values, turned).astype(BF16), jnp.where(lower, turned, values).astype(BF16)]
    spread = jnp.concatenate(
        [jnp.concatenate([part * m for m in head_rows], axis=1) for part in spread], axis=0
    )
    scores = lax.dot_general(keys, query, (((1,), (1,)), ((), ())), preferred_element_type=F32)
    scores = (scores * HD ** (-0.5) + bias).reshape(HEADS, WIN * WIN, 2 * WIN * WIN)
    powers = jnp.exp(scores - jnp.max(scores, axis=1, keepdims=True))
    probs = powers * (1.0 / jnp.sum(powers, axis=1, keepdims=True))
    probs = probs.reshape(HEADS * WIN * WIN, 2 * WIN * WIN).astype(BF16)
    both = jnp.dot(spread, probs, preferred_element_type=F32)
    return jnp.where(lower, both[:C], both[C:]).astype(BF16)


def kernel(
    ny, nx, height, breadth,
    feat_in, again_in, tw_in, ow_in, table_in, hgain_in, ew_in, sw_in, out_ref,
    feat, again, tw, ow, table, hgain, ew, sw, out,
    first, ext, back, bias, wide_rows, vt, cs, cr, bcs, bcr, rs, rr, brs, brr, ds, dr, bds, bdr,
    ssem, rsem, isem, osem,
):
    loads = [
        pltpu.make_async_copy(src, dst, isem.at[k])
        for k, (src, dst) in enumerate(
            [
                (table_in, table), (feat_in, feat), (again_in, again), (tw_in, tw),
                (ow_in, ow), (hgain_in, hgain), (ew_in, ew), (sw_in, sw),
            ]
        )
    ]
    for load in loads:
        load.start()
    gy, gx = lax.axis_index("gy"), lax.axis_index("gx")
    up, down = lax.rem(gy + ny - 1, ny), lax.rem(gy + 1, ny)
    left, right = lax.rem(gx + nx - 1, nx), lax.rem(gx + 1, nx)
    barrier = pltpu.get_barrier_semaphore()
    around = [(up, gx), (gy, left), (up, left), (down, gx), (gy, right), (down, right)]
    for who in around:
        pl.semaphore_signal(barrier, inc=1, device_id=who, device_id_type=pl.DeviceIdType.MESH)

    jj = lax.broadcasted_iota(jnp.int32, (WIN, 2 * WIN * WIN), 0)
    lane = lax.broadcasted_iota(jnp.int32, (WIN, 2 * WIN * WIN), 1)
    col_cut = ((jj >= SHIFT) != (lane & 7 >= SHIFT)) & (lane >= WIN * WIN) & (gx == nx - 1)
    extent = 2 * WIN - 1
    entry = lax.broadcasted_iota(jnp.int32, (extent * extent, 2 * WIN * WIN), 0)
    place = lax.broadcasted_iota(jnp.int32, (extent * extent, 2 * WIN * WIN), 1)
    target = entry - ((place >> 3) * extent + (place & 7) + WIN - 1)
    loads[0].wait()
    rest = jnp.concatenate([table[0], table[1]], axis=0)
    terms = []
    for _ in range(3):
        terms.append(rest.astype(BF16).astype(F32))
        rest = rest - terms[-1]
    terms = jnp.concatenate(terms, axis=0).astype(BF16)
    for x in range(WIN):
        pick = jnp.where(target == -x, 1.0, 0.0).astype(BF16)
        found = jnp.dot(terms, pick, preferred_element_type=F32)
        wide_rows[x] = found[:WIN] + found[WIN : 2 * WIN] + found[2 * WIN :]
    for b in range(2):
        for h in range(HEADS):
            rows = wide_rows[:, b * HEADS + h, :]
            for y in range(WIN):
                at = (WIN - 1 - y) * WIN
                piece = jnp.where(
                    lane < WIN * WIN,
                    pltpu.roll(rows, (2 * WIN * WIN - at) % (2 * WIN * WIN), 1),
                    pltpu.roll(rows, (WIN * WIN - at) % (2 * WIN * WIN), 1),
                )
                spot = slice(h * 64 + y * WIN, h * 64 + (y + 1) * WIN)
                if b == 0:
                    bias[0, spot] = piece
                else:
                    row_cut = ((lane & 63 >= SHIFT * WIN) != (y >= SHIFT)) & (gy == ny - 1)
                    bias[1, spot] = piece + jnp.where(col_cut, -100.0, 0.0)
                    bias[2, spot] = piece + jnp.where(col_cut | row_cut, -100.0, 0.0)

    token = lax.broadcasted_iota(jnp.int32, (2 * WIN * WIN, C), 0)
    second = token >= WIN * WIN
    lane_of = lax.broadcasted_iota(jnp.int32, (C, 2 * WIN * WIN), 1)
    row_of = lax.broadcasted_iota(jnp.int32, (C, 2 * WIN * WIN), 0)
    lower = lane_of < WIN * WIN
    head_rows = [
        jnp.where((row_of >> 5) == 2 * k + (lane_of >> 6), 1.0, 0.0).astype(BF16) for k in range(2)
    ]
    channel = lax.broadcasted_iota(jnp.int32, (1, C), 1)
    heads = [jnp.where(channel >> 5 == h, 1.0, 0.0).astype(BF16) for h in range(HEADS)]
    bands = height // WIN
    band = 2 * WIN * WIN
    group = GROUP
    groups = bands // group
    tall = group * WIN

    def dot(a, b):
        return jnp.dot(a, b, preferred_element_type=F32)

    wide = 2 * group

    def spots(first_band, count):
        return [lax.rem(first_band + k, bands) for k in range(count)]

    def read(ref, r, c):
        return [ref[pl.ds(r, WIN), pl.ds(c + w * WIN, WIN), :].reshape(WIN * WIN, C) for w in range(2)]

    def write(ref, r, c, rows):
        for w in range(2):
            ref[pl.ds(r, WIN), pl.ds(c + w * WIN, WIN), :] = rows[
                w * WIN * WIN : (w + 1) * WIN * WIN
            ].reshape(WIN, WIN, C)

    def attend(x, b, biases):
        queries_keys = dot(x, tw[b, :, : 2 * C])
        branches = []
        for k, table_of in enumerate(biases):
            span = slice(k * band, (k + 1) * band)
            values = lax.dot_general(vt[b], x[span], (((1,), (1,)), ((), ())), preferred_element_type=F32)
            ctx = window_pair(
                queries_keys[span], values, bias[table_of], second, lower, heads, head_rows
            )
            branches.append(
                lax.dot_general(ctx, ow[b], (((0,), (0,)), ((), ())), preferred_element_type=F32)
            )
        return jnp.concatenate(branches, axis=0)

    def ffn(z, b):
        normed = layer_norm(z, hgain[b : b + 1]).astype(BF16)
        hidden = gelu(dot(normed, ew[b])).astype(BF16)
        return z + dot(hidden, sw[b])

    def block0(i, carry):
        places = spots(i * wide, wide)
        z = jnp.concatenate([part for r in places for part in read(feat, r * WIN, 0)], axis=0).astype(F32)
        branch = attend(layer_norm(z, again[0:1]).astype(BF16), 0, [0] * wide)
        z = ffn(z + branch.astype(BF16).astype(F32), 0)
        normed = layer_norm(z, again[1:2])
        for k, r in enumerate(places):
            write(first, r * WIN, 0, z[k * band : (k + 1) * band])
            write(ext, r * WIN, 0, normed[k * band : (k + 1) * band])
        return carry

    def remote(src, dst, k, who):
        return pltpu.make_async_remote_copy(
            src_ref=src, dst_ref=dst, send_sem=ssem.at[k], recv_sem=rsem.at[k],
            device_id=who, device_id_type=pl.DeviceIdType.MESH,
        )

    def column(g):
        return remote(cs.at[g], cr.at[g], g, (gy, left))

    def column_back(g):
        return remote(bcs.at[g], bcr.at[g], groups + g, (gy, right))

    strips = [
        remote(rs, rr, 2 * groups, (up, gx)), remote(ds, dr, 2 * groups + 1, (up, left)),
        remote(brs, brr, 2 * groups + 2, (down, gx)), remote(bds, bdr, 2 * groups + 3, (down, right)),
    ]
    half = tall // 2

    def pack(ref, r0, c0):
        low = ref[pl.ds(r0, half), c0 : c0 + SHIFT, :]
        high = ref[pl.ds(r0 + half, half), c0 : c0 + SHIFT, :]
        return jnp.concatenate([low, high], axis=1).reshape(half * WIN, C).astype(BF16)

    def unpack(ref, r0, c0, buf):
        both = buf.astype(F32).reshape(half, WIN, C)
        ref[pl.ds(r0, half), c0 : c0 + SHIFT, :] = both[:, :SHIFT]
        ref[pl.ds(r0 + half, half), c0 : c0 + SHIFT, :] = both[:, SHIFT:]

    for load in loads[1:]:
        load.wait()
    for b in range(2):
        vt[b] = tw[b, :, 2 * C :].astype(F32).T.astype(BF16)

    def step0(i, carry):
        block0(i, carry)
        for k in range(2):
            cs[2 * i + k] = pack(ext, (2 * i + k) * tall, 0)

        @pl.when(i == 0)
        def _():
            rs[...] = ext[0:SHIFT, 0:breadth, :].reshape(SHIFT * breadth, C).astype(BF16)
            ds[...] = ext[0:SHIFT, 0:WIN, :].reshape(SHIFT * WIN, C).astype(BF16)
            pl.semaphore_wait(barrier, 6)
            strips[0].start()
            strips[1].start()

        for k in range(2):
            column(2 * i + k).start()
        return carry

    lax.fori_loop(0, groups // 2, step0, 0)

    def block1(i, carry):
        places = spots(i * group, group)
        x = jnp.concatenate([part for r in places for part in read(ext, r * WIN + SHIFT, SHIFT)], axis=0)
        branch = attend(x.astype(BF16), 1, [jnp.where(r == bands - 1, 2, 1) for r in places])
        for k, r in enumerate(places):
            write(back, r * WIN + SHIFT, SHIFT, branch[k * band : (k + 1) * band])
        return carry

    def enter(g):
        column(g).wait()
        unpack(ext, g * tall, breadth, cr[g])

    def step1(g, carry):
        @pl.when(g == 0)
        def _():
            enter(g)

        @pl.when(g < groups - 1)
        def _():
            enter(g + 1)

        @pl.when(g == groups - 1)
        def _():
            strips[0].wait()
            strips[1].wait()
            ext[height : height + SHIFT, 0:breadth, :] = rr[...].astype(F32).reshape(SHIFT, breadth, C)
            ext[height : height + SHIFT, breadth : breadth + SHIFT, :] = (
                dr[...].astype(F32).reshape(SHIFT, WIN, C)[:, :SHIFT]
            )

        block1(g, carry)
        bcs[g] = pack(back, g * tall + SHIFT, breadth)
        column_back(g).start()

        @pl.when(g == groups - 1)
        def _():
            brs[...] = back[height : height + SHIFT, 0:breadth, :].reshape(SHIFT * breadth, C).astype(BF16)
            bds[...] = (
                back[height : height + SHIFT, breadth : breadth + WIN, :].reshape(SHIFT * WIN, C).astype(BF16)
            )
            strips[2].start()
            strips[3].start()

        return carry

    lax.fori_loop(0, groups, step1, 0)

    def arrive(g):
        column_back(g).wait()
        unpack(back, g * tall + SHIFT, 0, bcr[g])

    def tail(i, carry):
        places = spots(i * wide + group, wide)
        z = jnp.concatenate(
            [
                (
                    first[pl.ds(r * WIN, WIN), pl.ds(0, 2 * WIN), :]
                    + back[pl.ds(r * WIN, WIN), pl.ds(0, 2 * WIN), :].astype(BF16).astype(F32)
                ).reshape(band, C)
                for r in places
            ],
            axis=0,
        )
        z = ffn(z, 1)
        for k, r in enumerate(places):
            out[pl.ds(r * WIN, WIN), pl.ds(0, 2 * WIN), :] = z[k * band : (k + 1) * band].reshape(
                WIN, 2 * WIN, C
            )
        return carry

    def store(g):
        rows = pl.ds(pl.multiple_of(g * tall, tall), tall)
        return pltpu.make_async_copy(out.at[rows], out_ref.at[rows], osem.at[g])

    def step2(i, carry):
        @pl.when(i == 0)
        def _():
            arrive(0)

        arrive(2 * i + 1)

        @pl.when(i < groups // 2 - 1)
        def _():
            arrive(2 * i + 2)

        @pl.when(i == groups // 2 - 1)
        def _():
            strips[2].wait()
            strips[3].wait()
            back[0:SHIFT, 0:breadth, :] = brr[...].astype(F32).reshape(SHIFT, breadth, C)
            back[0:SHIFT, 0:SHIFT, :] = bdr[...].astype(F32).reshape(SHIFT, WIN, C)[:, :SHIFT]

        tail(i, carry)
        store(2 * i + 1).start()
        store(lax.rem(2 * i + 2, groups)).start()
        return carry

    lax.fori_loop(0, groups // 2, step2, 0)
    for g in range(groups):
        store(g).wait()


def on_device(ny, nx, *operands):
    height, breadth, _ = operands[0].shape
    groups = height // (GROUP * WIN)
    col, row, corner = (groups, GROUP * WIN * SHIFT, C), (SHIFT * breadth, C), (SHIFT * WIN, C)
    hbm = pl.BlockSpec(memory_space=pl.ANY)
    return pl.pallas_call(
        functools.partial(kernel, ny, nx, height, breadth),
        out_shape=jax.ShapeDtypeStruct((height, breadth, C), F32),
        in_specs=[hbm] * len(operands),
        out_specs=hbm,
        scratch_shapes=[pltpu.VMEM(x.shape, x.dtype) for x in operands]
        + [
            pltpu.VMEM((height, breadth, C), F32),
            pltpu.VMEM((height, breadth, C), F32),
            pltpu.VMEM((height + SHIFT, breadth + WIN, C), F32),
            pltpu.VMEM((height + SHIFT, breadth + WIN, C), F32),
            pltpu.VMEM((3, HEADS * WIN * WIN, 2 * WIN * WIN), F32),
            pltpu.VMEM((WIN, 2 * HEADS, 2 * WIN * WIN), F32),
            pltpu.VMEM((2, C, C), BF16),
        ]
        + [pltpu.VMEM(shape, BF16) for shape in [col] * 4 + [row] * 4 + [corner] * 4]
        + [
            pltpu.SemaphoreType.DMA((2 * groups + 4,)),
            pltpu.SemaphoreType.DMA((2 * groups + 4,)),
            pltpu.SemaphoreType.DMA((len(operands),)),
            pltpu.SemaphoreType.DMA((groups,)),
        ],
        compiler_params=pltpu.CompilerParams(
            collective_id=0, has_side_effects=True, vmem_limit_bytes=64 * 1024 * 1024
        ),
        cost_estimate=pl.CostEstimate(flops=10**9, bytes_accessed=2 * 10**6, transcendentals=10**6),
    )(*operands)


def solution(mesh):
    return jax.shard_map(
        functools.partial(on_device, mesh.shape["gy"], mesh.shape["gx"]),
        mesh=mesh,
        in_specs=(P("gy", "gx", None), P(), P(), P(), P(), P(), P(), P()),
        out_specs=P("gy", "gx", None),
        check_vma=False,
    )
```

```python
import functools

import jax
import jax.numpy as jnp
from jax import lax
from jax.experimental import pallas as pl
from jax.experimental.pallas import tpu as pltpu
from jax.sharding import PartitionSpec as P

C = 128
HEADS = 4
WIN = 8
HD = 32
SHIFT = 4
EPSILON = 1e-05
F32 = jnp.float32
BF16 = jnp.bfloat16
GROUP = 2


def layer_norm(values, gain):
    center = values - jnp.mean(values, axis=-1, keepdims=True)
    spread = jnp.mean(center * center, axis=-1, keepdims=True)
    return center * lax.rsqrt(spread + EPSILON) * gain


ERFC = (0.254829592, -0.284496736, 1.421413741, -1.453152027, 1.061405429)
RATE = 0.3275911
POLE = 2**0.5 / RATE
TAIL = [0.5 * c * POLE ** (n + 1) for n, c in enumerate(ERFC)]


def gelu(x):
    a = jnp.abs(x)
    d = a + POLE
    t = pl.reciprocal(d, approx=True)
    t = t * (2.0 - d * t)
    poly = TAIL[4] * t + TAIL[3]
    for coef in TAIL[2::-1]:
        poly = poly * t + coef
    gauss = jnp.exp2((x * x) * (-0.5 * 1.4426950408889634))
    return jnp.maximum(x, 0.0) - (a * t) * (poly * gauss)


def window_pair(triple, bias, second, heads):
    triple = triple.reshape(WIN, 2 * WIN, 3 * C)
    query = triple[:, :, :C].reshape(2 * WIN * WIN, C)
    zero = jnp.zeros_like(query)
    query = jnp.concatenate(
        [jnp.where(second, zero, query), jnp.where(second, query, zero)], axis=1
    ).astype(BF16)
    keys, values = [], []
    for w in range(2):
        part = triple[:, w * WIN : (w + 1) * WIN, C:].reshape(WIN * WIN, 2 * C).astype(BF16)
        keys.append(jnp.concatenate([part[:, :C] * m for m in heads], axis=0))
        values.append(jnp.concatenate([part[:, C:] * m for m in heads], axis=0))
    keys = jnp.concatenate(keys, axis=1)
    values = jnp.concatenate(values, axis=1)
    scores = lax.dot_general(keys, query, (((1,), (1,)), ((), ())), preferred_element_type=F32)
    scores = (scores * HD ** (-0.5) + bias).reshape(HEADS, WIN * WIN, 2 * WIN * WIN)
    powers = jnp.exp(scores - jnp.max(scores, axis=1, keepdims=True))
    probs = powers * (1.0 / jnp.sum(powers, axis=1, keepdims=True))
    probs = probs.reshape(HEADS * WIN * WIN, 2 * WIN * WIN).astype(BF16)
    both = lax.dot_general(probs, values, (((0,), (0,)), ((), ())), preferred_element_type=F32)
    return jnp.where(second, both[:, C:], both[:, :C]).astype(BF16)


def kernel(
    ny, nx, height, breadth,
    feat_in, again_in, tw_in, ow_in, table_in, hgain_in, ew_in, sw_in, out_ref,
    feat, again, tw, ow, table, hgain, ew, sw, out,
    first, ext, back, bias, cs, cr, bcs, bcr, rs, rr, brs, brr, ds, dr, bds, bdr,
    ssem, rsem, isem, osem,
):
    loads = [
        pltpu.make_async_copy(src, dst, isem.at[k])
        for k, (src, dst) in enumerate(
            [
                (table_in, table), (feat_in, feat), (again_in, again), (tw_in, tw),
                (ow_in, ow), (hgain_in, hgain), (ew_in, ew), (sw_in, sw),
            ]
        )
    ]
    for load in loads:
        load.start()
    gy, gx = lax.axis_index("gy"), lax.axis_index("gx")
    up, down = lax.rem(gy + ny - 1, ny), lax.rem(gy + 1, ny)
    left, right = lax.rem(gx + nx - 1, nx), lax.rem(gx + 1, nx)
    barrier = pltpu.get_barrier_semaphore()
    around = [(up, gx), (gy, left), (up, left), (down, gx), (gy, right), (down, right)]
    for who in around:
        pl.semaphore_signal(barrier, inc=1, device_id=who, device_id_type=pl.DeviceIdType.MESH)

    jj = lax.broadcasted_iota(jnp.int32, (WIN, 2 * WIN * WIN), 0)
    lane = lax.broadcasted_iota(jnp.int32, (WIN, 2 * WIN * WIN), 1)
    col_cut = ((jj >= SHIFT) != (lane & 7 >= SHIFT)) & (lane & 15 >= WIN) & (gx == nx - 1)
    extent = 2 * WIN - 1
    entry = lax.broadcasted_iota(jnp.int32, (extent * extent, 4 * WIN * WIN), 0)
    place = lax.broadcasted_iota(jnp.int32, (extent * extent, 4 * WIN * WIN), 1)
    pick = jnp.where(
        (entry == (place >> 4) * extent + (place & 15)) & ((place & 15) < extent), 1.0, 0.0
    )
    first_half = lax.broadcasted_iota(jnp.int32, (WIN, 4 * WIN * WIN), 1) & 15 < WIN
    loads[0].wait()
    spread_rows = [
        jnp.dot(table[b], pick, precision=lax.Precision.HIGHEST, preferred_element_type=F32) for b in range(2)
    ]
    for b in range(2):
        for h in range(HEADS):
            row = jnp.broadcast_to(spread_rows[b][h : h + 1], (WIN, 4 * WIN * WIN))
            rows = jnp.where(
                first_half,
                pltpu.roll(row, 4 * WIN * WIN - WIN + 1, 1, stride=1, stride_axis=0),
                pltpu.roll(row, 1, 1, stride=1, stride_axis=0),
            )
            for y in range(WIN):
                at = (WIN - 1 - y) * 2 * WIN
                piece = rows[:, at : at + 2 * WIN * WIN]
                spot = slice(h * 64 + y * WIN, h * 64 + (y + 1) * WIN)
                if b == 0:
                    bias[0, spot] = piece
                else:
                    row_cut = ((lane >= SHIFT * 2 * WIN) != (y >= SHIFT)) & (gy == ny - 1)
                    bias[1, spot] = piece + jnp.where(col_cut, -100.0, 0.0)
                    bias[2, spot] = piece + jnp.where(col_cut | row_cut, -100.0, 0.0)

    token = lax.broadcasted_iota(jnp.int32, (2 * WIN * WIN, C), 0)
    second = token & 15 >= WIN
    channel = lax.broadcasted_iota(jnp.int32, (1, C), 1)
    heads = [jnp.where(channel >> 5 == h, 1.0, 0.0).astype(BF16) for h in range(HEADS)]
    bands = height // WIN
    band = 2 * WIN * WIN
    group = GROUP
    groups = bands // group
    tall = group * WIN

    def dot(a, b):
        return jnp.dot(a, b, preferred_element_type=F32)

    wide = 2 * group

    def spots(first_band, count):
        return [lax.rem(first_band + k, bands) for k in range(count)]

    def ffn(z, b):
        parts = []
        for k in range(z.shape[0] // band):
            part = z[k * band : (k + 1) * band]
            normed = layer_norm(part, hgain[b : b + 1]).astype(BF16)
            hidden = gelu(dot(normed, ew[b])).astype(BF16)
            parts.append(part + dot(hidden, sw[b]))
        return jnp.concatenate(parts, axis=0)

    def block0(i, carry):
        places = spots(i * wide, wide)
        z = jnp.concatenate(
            [feat[pl.ds(r * WIN, WIN), pl.ds(0, 2 * WIN), :].reshape(band, C) for r in places], axis=0
        ).astype(F32)
        triple = dot(layer_norm(z, again[0:1]).astype(BF16), tw[0])
        ctx = [window_pair(triple[k * band : (k + 1) * band], bias[0], second, heads) for k in range(wide)]
        branch = dot(jnp.concatenate(ctx, axis=0), ow[0]).astype(BF16).astype(F32)
        z = ffn(z + branch, 0)
        normed = layer_norm(z, again[1:2])
        for k, r in enumerate(places):
            spot = (pl.ds(r * WIN, WIN), pl.ds(0, 2 * WIN), slice(None))
            first[spot] = z[k * band : (k + 1) * band].reshape(WIN, 2 * WIN, C)
            ext[spot] = normed[k * band : (k + 1) * band].reshape(WIN, 2 * WIN, C)
        return carry

    def remote(src, dst, k, who):
        return pltpu.make_async_remote_copy(
            src_ref=src, dst_ref=dst, send_sem=ssem.at[k], recv_sem=rsem.at[k],
            device_id=who, device_id_type=pl.DeviceIdType.MESH,
        )

    def column(g):
        return remote(cs.at[g], cr.at[g], g, (gy, left))

    def column_back(g):
        return remote(bcs.at[g], bcr.at[g], groups + g, (gy, right))

    strips = [
        remote(rs, rr, 2 * groups, (up, gx)), remote(ds, dr, 2 * groups + 1, (up, left)),
        remote(brs, brr, 2 * groups + 2, (down, gx)), remote(bds, bdr, 2 * groups + 3, (down, right)),
    ]
    half = tall // 2

    def pack(ref, r0, c0):
        low = ref[pl.ds(r0, half), c0 : c0 + SHIFT, :]
        high = ref[pl.ds(r0 + half, half), c0 : c0 + SHIFT, :]
        return jnp.concatenate([low, high], axis=1).reshape(half * WIN, C).astype(BF16)

    def unpack(ref, r0, c0, buf):
        both = buf.astype(F32).reshape(half, WIN, C)
        ref[pl.ds(r0, half), c0 : c0 + SHIFT, :] = both[:, :SHIFT]
        ref[pl.ds(r0 + half, half), c0 : c0 + SHIFT, :] = both[:, SHIFT:]

    for load in loads[1:]:
        load.wait()

    def step0(i, carry):
        block0(i, carry)
        for k in range(2):
            cs[2 * i + k] = pack(ext, (2 * i + k) * tall, 0)

        @pl.when(i == 0)
        def _():
            rs[...] = ext[0:SHIFT, 0:breadth, :].reshape(SHIFT * breadth, C).astype(BF16)
            ds[...] = ext[0:SHIFT, 0:WIN, :].reshape(SHIFT * WIN, C).astype(BF16)
            pl.semaphore_wait(barrier, 6)
            strips[0].start()
            strips[1].start()

        for k in range(2):
            column(2 * i + k).start()
        return carry

    lax.fori_loop(0, groups // 2, step0, 0)

    def block1(i, carry):
        places = spots(i * group, group)
        x = jnp.concatenate(
            [
                ext[pl.ds(r * WIN + SHIFT, WIN), pl.ds(SHIFT, 2 * WIN), :].reshape(band, C)
                for r in places
            ],
            axis=0,
        ).astype(BF16)
        triple = dot(x, tw[1])
        ctx = [
            window_pair(
                triple[k * band : (k + 1) * band],
                bias[jnp.where(r == bands - 1, 2, 1)],
                second, heads,
            )
            for k, r in enumerate(places)
        ]
        branch = dot(jnp.concatenate(ctx, axis=0), ow[1])
        for k, r in enumerate(places):
            back[pl.ds(r * WIN + SHIFT, WIN), pl.ds(SHIFT, 2 * WIN), :] = branch[
                k * band : (k + 1) * band
            ].reshape(WIN, 2 * WIN, C)
        return carry

    def enter(g):
        column(g).wait()
        unpack(ext, g * tall, breadth, cr[g])

    def step1(g, carry):
        @pl.when(g == 0)
        def _():
            enter(g)

        @pl.when(g < groups - 1)
        def _():
            enter(g + 1)

        @pl.when(g == groups - 1)
        def _():
            strips[0].wait()
            strips[1].wait()
            ext[height : height + SHIFT, 0:breadth, :] = rr[...].astype(F32).reshape(SHIFT, breadth, C)
            ext[height : height + SHIFT, breadth : breadth + SHIFT, :] = (
                dr[...].astype(F32).reshape(SHIFT, WIN, C)[:, :SHIFT]
            )

        block1(g, carry)
        bcs[g] = pack(back, g * tall + SHIFT, breadth)
        column_back(g).start()

        @pl.when(g == groups - 1)
        def _():
            brs[...] = back[height : height + SHIFT, 0:breadth, :].reshape(SHIFT * breadth, C).astype(BF16)
            bds[...] = (
                back[height : height + SHIFT, breadth : breadth + WIN, :].reshape(SHIFT * WIN, C).astype(BF16)
            )
            strips[2].start()
            strips[3].start()

        return carry

    lax.fori_loop(0, groups, step1, 0)

    def arrive(g):
        column_back(g).wait()
        unpack(back, g * tall + SHIFT, 0, bcr[g])

    def tail(i, carry):
        places = spots(i * wide + group, wide)
        z = jnp.concatenate(
            [
                (
                    first[pl.ds(r * WIN, WIN), pl.ds(0, 2 * WIN), :]
                    + back[pl.ds(r * WIN, WIN), pl.ds(0, 2 * WIN), :].astype(BF16).astype(F32)
                ).reshape(band, C)
                for r in places
            ],
            axis=0,
        )
        z = ffn(z, 1)
        for k, r in enumerate(places):
            out[pl.ds(r * WIN, WIN), pl.ds(0, 2 * WIN), :] = z[k * band : (k + 1) * band].reshape(
                WIN, 2 * WIN, C
            )
        return carry

    def store(g):
        rows = pl.ds(pl.multiple_of(g * tall, tall), tall)
        return pltpu.make_async_copy(out.at[rows], out_ref.at[rows], osem.at[g])

    def step2(i, carry):
        @pl.when(i == 0)
        def _():
            arrive(0)

        arrive(2 * i + 1)

        @pl.when(i < groups // 2 - 1)
        def _():
            arrive(2 * i + 2)

        @pl.when(i == groups // 2 - 1)
        def _():
            strips[2].wait()
            strips[3].wait()
            back[0:SHIFT, 0:breadth, :] = brr[...].astype(F32).reshape(SHIFT, breadth, C)
            back[0:SHIFT, 0:SHIFT, :] = bdr[...].astype(F32).reshape(SHIFT, WIN, C)[:, :SHIFT]

        tail(i, carry)
        store(2 * i + 1).start()
        store(lax.rem(2 * i + 2, groups)).start()
        return carry

    lax.fori_loop(0, groups // 2, step2, 0)
    for g in range(groups):
        store(g).wait()


def on_device(ny, nx, *operands):
    height, breadth, _ = operands[0].shape
    groups = height // (GROUP * WIN)
    col, row, corner = (groups, GROUP * WIN * SHIFT, C), (SHIFT * breadth, C), (SHIFT * WIN, C)
    hbm = pl.BlockSpec(memory_space=pl.ANY)
    return pl.pallas_call(
        functools.partial(kernel, ny, nx, height, breadth),
        out_shape=jax.ShapeDtypeStruct((height, breadth, C), F32),
        in_specs=[hbm] * len(operands),
        out_specs=hbm,
        scratch_shapes=[pltpu.VMEM(x.shape, x.dtype) for x in operands]
        + [
            pltpu.VMEM((height, breadth, C), F32),
            pltpu.VMEM((height, breadth, C), F32),
            pltpu.VMEM((height + SHIFT, breadth + WIN, C), F32),
            pltpu.VMEM((height + SHIFT, breadth + WIN, C), F32),
            pltpu.VMEM((3, HEADS * WIN * WIN, 2 * WIN * WIN), F32),
        ]
        + [pltpu.VMEM(shape, BF16) for shape in [col] * 4 + [row] * 4 + [corner] * 4]
        + [
            pltpu.SemaphoreType.DMA((2 * groups + 4,)),
            pltpu.SemaphoreType.DMA((2 * groups + 4,)),
            pltpu.SemaphoreType.DMA((len(operands),)),
            pltpu.SemaphoreType.DMA((groups,)),
        ],
        compiler_params=pltpu.CompilerParams(
            collective_id=0, has_side_effects=True, vmem_limit_bytes=64 * 1024 * 1024
        ),
        cost_estimate=pl.CostEstimate(flops=10**9, bytes_accessed=2 * 10**6, transcendentals=10**6),
    )(*operands)


def solution(mesh):
    return jax.shard_map(
        functools.partial(on_device, mesh.shape["gy"], mesh.shape["gx"]),
        mesh=mesh,
        in_specs=(P("gy", "gx", None), P(), P(), P(), P(), P(), P(), P()),
        out_specs=P("gy", "gx", None),
        check_vma=False,
    )
```

```python
import functools

import jax
import jax.numpy as jnp
from jax import lax
from jax.experimental import pallas as pl
from jax.experimental.pallas import tpu as pltpu
from jax.sharding import PartitionSpec as P

C = 128
HEADS = 4
WIN = 8
HD = 32
SHIFT = 4
EPSILON = 1e-05
F32 = jnp.float32
BF16 = jnp.bfloat16
GROUP = 2


def layer_norm(values, gain):
    center = values - jnp.mean(values, axis=-1, keepdims=True)
    spread = jnp.mean(center * center, axis=-1, keepdims=True)
    return center * lax.rsqrt(spread + EPSILON) * gain


ERFC = (0.254829592, -0.284496736, 1.421413741, -1.453152027, 1.061405429)
RATE = 0.3275911
POLE = 2**0.5 / RATE
TAIL = [0.5 * c * POLE ** (n + 1) for n, c in enumerate(ERFC)]


def gelu(x):
    a = jnp.abs(x)
    d = a + POLE
    t = pl.reciprocal(d, approx=True)
    t = t * (2.0 - d * t)
    poly = TAIL[4] * t + TAIL[3]
    for coef in TAIL[2::-1]:
        poly = poly * t + coef
    gauss = jnp.exp2((x * x) * (-0.5 * 1.4426950408889634))
    return jnp.maximum(x, 0.0) - (a * t) * (poly * gauss)


def window_pair(triple, bias, second, heads):
    triple = triple.reshape(WIN, 2 * WIN, 3 * C)
    query = triple[:, :, :C].reshape(2 * WIN * WIN, C)
    zero = jnp.zeros_like(query)
    query = jnp.concatenate(
        [jnp.where(second, zero, query), jnp.where(second, query, zero)], axis=1
    ).astype(BF16)
    keys, values = [], []
    for w in range(2):
        part = triple[:, w * WIN : (w + 1) * WIN, C:].reshape(WIN * WIN, 2 * C).astype(BF16)
        keys.append(jnp.concatenate([part[:, :C] * m for m in heads], axis=0))
        values.append(jnp.concatenate([part[:, C:] * m for m in heads], axis=0))
    keys = jnp.concatenate(keys, axis=1)
    values = jnp.concatenate(values, axis=1)
    scores = lax.dot_general(keys, query, (((1,), (1,)), ((), ())), preferred_element_type=F32)
    scores = (scores * HD ** (-0.5) + bias).reshape(HEADS, WIN * WIN, 2 * WIN * WIN)
    powers = jnp.exp(scores - jnp.max(scores, axis=1, keepdims=True))
    probs = powers * (1.0 / jnp.sum(powers, axis=1, keepdims=True))
    probs = probs.reshape(HEADS * WIN * WIN, 2 * WIN * WIN).astype(BF16)
    both = lax.dot_general(probs, values, (((0,), (0,)), ((), ())), preferred_element_type=F32)
    return jnp.where(second, both[:, C:], both[:, :C]).astype(BF16)


def kernel(
    ny, nx, height, breadth,
    feat_in, again_in, tw_in, ow_in, table_in, hgain_in, ew_in, sw_in, middle_ref, out_ref,
    feat, again, tw, ow, table, hgain, ew, sw, out,
    first, ext, back, bias, cs, cr, bcs, bcr, rs, rr, brs, brr, ds, dr, bds, bdr,
    ssem, rsem, isem, osem,
):
    loads = [
        pltpu.make_async_copy(src, dst, isem.at[k])
        for k, (src, dst) in enumerate(
            [
                (table_in, table), (feat_in, feat), (again_in, again), (tw_in, tw),
                (ow_in, ow), (hgain_in, hgain), (ew_in, ew), (sw_in, sw),
            ]
        )
    ]
    for load in loads:
        load.start()
    gy, gx = lax.axis_index("gy"), lax.axis_index("gx")
    up, down = lax.rem(gy + ny - 1, ny), lax.rem(gy + 1, ny)
    left, right = lax.rem(gx + nx - 1, nx), lax.rem(gx + 1, nx)
    barrier = pltpu.get_barrier_semaphore()
    around = [(up, gx), (gy, left), (up, left), (down, gx), (gy, right), (down, right)]
    for who in around:
        pl.semaphore_signal(barrier, inc=1, device_id=who, device_id_type=pl.DeviceIdType.MESH)

    jj = lax.broadcasted_iota(jnp.int32, (WIN, 2 * WIN * WIN), 0)
    lane = lax.broadcasted_iota(jnp.int32, (WIN, 2 * WIN * WIN), 1)
    col_cut = ((jj >= SHIFT) != (lane & 7 >= SHIFT)) & (lane & 15 >= WIN) & (gx == nx - 1)
    extent = 2 * WIN - 1
    entry = lax.broadcasted_iota(jnp.int32, (extent * extent, 4 * WIN * WIN), 0)
    place = lax.broadcasted_iota(jnp.int32, (extent * extent, 4 * WIN * WIN), 1)
    pick = jnp.where(
        (entry == (place >> 4) * extent + (place & 15)) & ((place & 15) < extent), 1.0, 0.0
    )
    first_half = lax.broadcasted_iota(jnp.int32, (WIN, 4 * WIN * WIN), 1) & 15 < WIN
    loads[0].wait()
    spread_rows = [
        jnp.dot(table[b], pick, precision=lax.Precision.HIGHEST, preferred_element_type=F32) for b in range(2)
    ]
    for b in range(2):
        for h in range(HEADS):
            row = jnp.broadcast_to(spread_rows[b][h : h + 1], (WIN, 4 * WIN * WIN))
            rows = jnp.where(
                first_half,
                pltpu.roll(row, 4 * WIN * WIN - WIN + 1, 1, stride=1, stride_axis=0),
                pltpu.roll(row, 1, 1, stride=1, stride_axis=0),
            )
            for y in range(WIN):
                at = (WIN - 1 - y) * 2 * WIN
                piece = rows[:, at : at + 2 * WIN * WIN]
                spot = slice(h * 64 + y * WIN, h * 64 + (y + 1) * WIN)
                if b == 0:
                    bias[0, spot] = piece
                else:
                    row_cut = ((lane >= SHIFT * 2 * WIN) != (y >= SHIFT)) & (gy == ny - 1)
                    bias[1, spot] = piece + jnp.where(col_cut, -100.0, 0.0)
                    bias[2, spot] = piece + jnp.where(col_cut | row_cut, -100.0, 0.0)

    token = lax.broadcasted_iota(jnp.int32, (2 * WIN * WIN, C), 0)
    second = token & 15 >= WIN
    channel = lax.broadcasted_iota(jnp.int32, (1, C), 1)
    heads = [jnp.where(channel >> 5 == h, 1.0, 0.0).astype(BF16) for h in range(HEADS)]
    bands = height // WIN
    band = 2 * WIN * WIN
    group = GROUP
    groups = bands // group
    tall = group * WIN

    def dot(a, b):
        return jnp.dot(a, b, preferred_element_type=F32)

    wide = 2 * group

    def spots(first_band, count):
        return [lax.rem(first_band + k, bands) for k in range(count)]

    def ffn(z, b):
        normed = layer_norm(z, hgain[b : b + 1]).astype(BF16)
        hidden = gelu(dot(normed, ew[b])).astype(BF16)
        return dot(hidden, sw[b])

    def block0(i, carry):
        places = spots(i * wide, wide)
        z = jnp.concatenate(
            [feat[pl.ds(r * WIN, WIN), pl.ds(0, 2 * WIN), :].reshape(band, C) for r in places], axis=0
        ).astype(F32)
        triple = dot(layer_norm(z, again[0:1]).astype(BF16), tw[0])
        ctx = [window_pair(triple[k * band : (k + 1) * band], bias[0], second, heads) for k in range(wide)]
        branch = dot(jnp.concatenate(ctx, axis=0), ow[0]).astype(BF16).astype(F32)
        z = z + branch
        z = z + ffn(z, 0)
        normed = layer_norm(z, again[1:2])
        for k, r in enumerate(places):
            spot = (pl.ds(r * WIN, WIN), pl.ds(0, 2 * WIN), slice(None))
            first[spot] = z[k * band : (k + 1) * band].reshape(WIN, 2 * WIN, C)
            ext[spot] = normed[k * band : (k + 1) * band].reshape(WIN, 2 * WIN, C)
        return carry

    def remote(src, dst, k, who):
        return pltpu.make_async_remote_copy(
            src_ref=src, dst_ref=dst, send_sem=ssem.at[k], recv_sem=rsem.at[k],
            device_id=who, device_id_type=pl.DeviceIdType.MESH,
        )

    def column(g):
        return remote(cs.at[g], cr.at[g], g, (gy, left))

    def column_back(g):
        return remote(bcs.at[g], bcr.at[g], groups + g, (gy, right))

    strips = [
        remote(rs, rr, 2 * groups, (up, gx)), remote(ds, dr, 2 * groups + 1, (up, left)),
        remote(brs, brr, 2 * groups + 2, (down, gx)), remote(bds, bdr, 2 * groups + 3, (down, right)),
    ]
    half = tall // 2

    def pack(ref, r0, c0):
        low = ref[pl.ds(r0, half), c0 : c0 + SHIFT, :]
        high = ref[pl.ds(r0 + half, half), c0 : c0 + SHIFT, :]
        return jnp.concatenate([low, high], axis=1).reshape(half * WIN, C).astype(BF16)

    def unpack(ref, r0, c0, buf):
        both = buf.astype(F32).reshape(half, WIN, C)
        ref[pl.ds(r0, half), c0 : c0 + SHIFT, :] = both[:, :SHIFT]
        ref[pl.ds(r0 + half, half), c0 : c0 + SHIFT, :] = both[:, SHIFT:]

    for load in loads[1:]:
        load.wait()

    def step0(i, carry):
        block0(i, carry)
        for k in range(2):
            cs[2 * i + k] = pack(ext, (2 * i + k) * tall, 0)

        @pl.when(i == 0)
        def _():
            rs[...] = ext[0:SHIFT, 0:breadth, :].reshape(SHIFT * breadth, C).astype(BF16)
            ds[...] = ext[0:SHIFT, 0:WIN, :].reshape(SHIFT * WIN, C).astype(BF16)
            pl.semaphore_wait(barrier, 6)
            strips[0].start()
            strips[1].start()

        for k in range(2):
            column(2 * i + k).start()
        return carry

    lax.fori_loop(0, groups // 2, step0, 0)

    def block1(i, carry):
        places = spots(i * group, group)
        x = jnp.concatenate(
            [
                ext[pl.ds(r * WIN + SHIFT, WIN), pl.ds(SHIFT, 2 * WIN), :].reshape(band, C)
                for r in places
            ],
            axis=0,
        ).astype(BF16)
        triple = dot(x, tw[1])
        ctx = [
            window_pair(
                triple[k * band : (k + 1) * band],
                bias[jnp.where(r == bands - 1, 2, 1)],
                second, heads,
            )
            for k, r in enumerate(places)
        ]
        branch = dot(jnp.concatenate(ctx, axis=0), ow[1])
        for k, r in enumerate(places):
            back[pl.ds(r * WIN + SHIFT, WIN), pl.ds(SHIFT, 2 * WIN), :] = branch[
                k * band : (k + 1) * band
            ].reshape(WIN, 2 * WIN, C)
        return carry

    def enter(g):
        column(g).wait()
        unpack(ext, g * tall, breadth, cr[g])

    def step1(g, carry):
        @pl.when(g == 0)
        def _():
            enter(g)

        @pl.when(g < groups - 1)
        def _():
            enter(g + 1)

        @pl.when(g == groups - 1)
        def _():
            strips[0].wait()
            strips[1].wait()
            ext[height : height + SHIFT, 0:breadth, :] = rr[...].astype(F32).reshape(SHIFT, breadth, C)
            ext[height : height + SHIFT, breadth : breadth + SHIFT, :] = (
                dr[...].astype(F32).reshape(SHIFT, WIN, C)[:, :SHIFT]
            )

        block1(g, carry)
        bcs[g] = pack(back, g * tall + SHIFT, breadth)
        column_back(g).start()

        @pl.when(g == groups - 1)
        def _():
            brs[...] = back[height : height + SHIFT, 0:breadth, :].reshape(SHIFT * breadth, C).astype(BF16)
            bds[...] = (
                back[height : height + SHIFT, breadth : breadth + WIN, :].reshape(SHIFT * WIN, C).astype(BF16)
            )
            strips[2].start()
            strips[3].start()

        return carry

    lax.fori_loop(0, groups, step1, 0)

    def arrive(g):
        column_back(g).wait()
        unpack(back, g * tall + SHIFT, 0, bcr[g])

    def tail(i, carry):
        places = spots(i * wide + group, wide)
        z = jnp.concatenate(
            [
                (
                    first[pl.ds(r * WIN, WIN), pl.ds(0, 2 * WIN), :]
                    + back[pl.ds(r * WIN, WIN), pl.ds(0, 2 * WIN), :].astype(BF16).astype(F32)
                ).reshape(band, C)
                for r in places
            ],
            axis=0,
        )
        change = ffn(z, 1)
        for k, r in enumerate(places):
            spot = (pl.ds(r * WIN, WIN), pl.ds(0, 2 * WIN), slice(None))
            first[spot] = z[k * band : (k + 1) * band].reshape(WIN, 2 * WIN, C)
            out[spot] = change[k * band : (k + 1) * band].reshape(WIN, 2 * WIN, C)
        return carry

    def store(g):
        rows = pl.ds(pl.multiple_of(g * tall, tall), tall)
        return [
            pltpu.make_async_copy(first.at[rows], middle_ref.at[rows], osem.at[g]),
            pltpu.make_async_copy(out.at[rows], out_ref.at[rows], osem.at[groups + g]),
        ]

    def step2(i, carry):
        @pl.when(i == 0)
        def _():
            arrive(0)

        arrive(2 * i + 1)

        @pl.when(i < groups // 2 - 1)
        def _():
            arrive(2 * i + 2)

        @pl.when(i == groups // 2 - 1)
        def _():
            strips[2].wait()
            strips[3].wait()
            back[0:SHIFT, 0:breadth, :] = brr[...].astype(F32).reshape(SHIFT, breadth, C)
            back[0:SHIFT, 0:SHIFT, :] = bdr[...].astype(F32).reshape(SHIFT, WIN, C)[:, :SHIFT]

        tail(i, carry)
        for copy in store(2 * i + 1) + store(lax.rem(2 * i + 2, groups)):
            copy.start()
        return carry

    lax.fori_loop(0, groups // 2, step2, 0)
    for g in range(groups):
        for copy in store(g):
            copy.wait()


def on_device(ny, nx, *operands):
    height, breadth, _ = operands[0].shape
    groups = height // (GROUP * WIN)
    col, row, corner = (groups, GROUP * WIN * SHIFT, C), (SHIFT * breadth, C), (SHIFT * WIN, C)
    hbm = pl.BlockSpec(memory_space=pl.ANY)
    middle, change = pl.pallas_call(
        functools.partial(kernel, ny, nx, height, breadth),
        out_shape=[jax.ShapeDtypeStruct((height, breadth, C), F32)] * 2,
        in_specs=[hbm] * len(operands),
        out_specs=[hbm] * 2,
        scratch_shapes=[pltpu.VMEM(x.shape, x.dtype) for x in operands]
        + [
            pltpu.VMEM((height, breadth, C), F32),
            pltpu.VMEM((height, breadth, C), F32),
            pltpu.VMEM((height + SHIFT, breadth + WIN, C), F32),
            pltpu.VMEM((height + SHIFT, breadth + WIN, C), F32),
            pltpu.VMEM((3, HEADS * WIN * WIN, 2 * WIN * WIN), F32),
        ]
        + [pltpu.VMEM(shape, BF16) for shape in [col] * 4 + [row] * 4 + [corner] * 4]
        + [
            pltpu.SemaphoreType.DMA((2 * groups + 4,)),
            pltpu.SemaphoreType.DMA((2 * groups + 4,)),
            pltpu.SemaphoreType.DMA((len(operands),)),
            pltpu.SemaphoreType.DMA((2 * groups,)),
        ],
        compiler_params=pltpu.CompilerParams(
            collective_id=0, has_side_effects=True, vmem_limit_bytes=64 * 1024 * 1024
        ),
        cost_estimate=pl.CostEstimate(flops=10**9, bytes_accessed=2 * 10**6, transcendentals=10**6),
    )(*operands)
    return middle + change


def solution(mesh):
    return jax.shard_map(
        functools.partial(on_device, mesh.shape["gy"], mesh.shape["gx"]),
        mesh=mesh,
        in_specs=(P("gy", "gx", None), P(), P(), P(), P(), P(), P(), P()),
        out_specs=P("gy", "gx", None),
        check_vma=False,
    )
```

```python
import functools

import jax
import jax.numpy as jnp
from jax import lax
from jax.experimental import pallas as pl
from jax.experimental.pallas import tpu as pltpu
from jax.sharding import PartitionSpec as P

C = 128
HEADS = 4
WIN = 8
HD = 32
SHIFT = 4
EPSILON = 1e-05
F32 = jnp.float32
BF16 = jnp.bfloat16
GROUP = 2


def layer_norm(values, gain):
    center = values - jnp.mean(values, axis=-1, keepdims=True)
    spread = jnp.mean(center * center, axis=-1, keepdims=True)
    return center * lax.rsqrt(spread + EPSILON) * gain


ERFC = (0.254829592, -0.284496736, 1.421413741, -1.453152027, 1.061405429)
RATE = 0.3275911
POLE = 2**0.5 / RATE
TAIL = [0.5 * c * POLE ** (n + 1) for n, c in enumerate(ERFC)]


def gelu(x):
    a = jnp.abs(x)
    d = a + POLE
    t = pl.reciprocal(d, approx=True)
    t = t * (2.0 - d * t)
    poly = TAIL[4] * t + TAIL[3]
    for coef in TAIL[2::-1]:
        poly = poly * t + coef
    gauss = jnp.exp2((x * x) * (-0.5 * 1.4426950408889634))
    return jnp.maximum(x, 0.0) - (a * t) * (poly * gauss)


def window_pair(triple, bias, second, heads):
    triple = triple.reshape(WIN, 2 * WIN, 3 * C)
    query = triple[:, :, :C].reshape(2 * WIN * WIN, C)
    zero = jnp.zeros_like(query)
    query = jnp.concatenate(
        [jnp.where(second, zero, query), jnp.where(second, query, zero)], axis=1
    ).astype(BF16)
    keys, values = [], []
    for w in range(2):
        part = triple[:, w * WIN : (w + 1) * WIN, C:].reshape(WIN * WIN, 2 * C).astype(BF16)
        keys.append(jnp.concatenate([part[:, :C] * m for m in heads], axis=0))
        values.append(jnp.concatenate([part[:, C:] * m for m in heads], axis=0))
    keys = jnp.concatenate(keys, axis=1)
    values = jnp.concatenate(values, axis=1)
    scores = lax.dot_general(keys, query, (((1,), (1,)), ((), ())), preferred_element_type=F32)
    scores = (scores * HD ** (-0.5) + bias).reshape(HEADS, WIN * WIN, 2 * WIN * WIN)
    powers = jnp.exp(scores - jnp.max(scores, axis=1, keepdims=True))
    probs = powers * (1.0 / jnp.sum(powers, axis=1, keepdims=True))
    probs = probs.reshape(HEADS * WIN * WIN, 2 * WIN * WIN).astype(BF16)
    both = lax.dot_general(probs, values, (((0,), (0,)), ((), ())), preferred_element_type=F32)
    return jnp.where(second, both[:, C:], both[:, :C]).astype(BF16)


def kernel(
    ny, nx, height, breadth,
    feat_in, again_in, tw_in, ow_in, table_in, hgain_in, ew_in, sw_in, out,
    feat, again, tw, ow, table, hgain, ew, sw,
    first, ext, back, bias, cs, cr, bcs, bcr, rs, rr, brs, brr, ds, dr, bds, bdr,
    ssem, rsem, isem,
):
    loads = [
        pltpu.make_async_copy(src, dst, isem.at[k])
        for k, (src, dst) in enumerate(
            [
                (table_in, table), (feat_in, feat), (again_in, again), (tw_in, tw),
                (ow_in, ow), (hgain_in, hgain), (ew_in, ew), (sw_in, sw),
            ]
        )
    ]
    for load in loads:
        load.start()
    gy, gx = lax.axis_index("gy"), lax.axis_index("gx")
    up, down = lax.rem(gy + ny - 1, ny), lax.rem(gy + 1, ny)
    left, right = lax.rem(gx + nx - 1, nx), lax.rem(gx + 1, nx)
    barrier = pltpu.get_barrier_semaphore()
    around = [(up, gx), (gy, left), (up, left), (down, gx), (gy, right), (down, right)]
    for who in around:
        pl.semaphore_signal(barrier, inc=1, device_id=who, device_id_type=pl.DeviceIdType.MESH)

    jj = lax.broadcasted_iota(jnp.int32, (WIN, 2 * WIN * WIN), 0)
    lane = lax.broadcasted_iota(jnp.int32, (WIN, 2 * WIN * WIN), 1)
    col_cut = ((jj >= SHIFT) != (lane & 7 >= SHIFT)) & (lane & 15 >= WIN) & (gx == nx - 1)
    extent = 2 * WIN - 1
    entry = lax.broadcasted_iota(jnp.int32, (extent * extent, 4 * WIN * WIN), 0)
    place = lax.broadcasted_iota(jnp.int32, (extent * extent, 4 * WIN * WIN), 1)
    pick = jnp.where(
        (entry == (place >> 4) * extent + (place & 15)) & ((place & 15) < extent), 1.0, 0.0
    )
    first_half = lax.broadcasted_iota(jnp.int32, (WIN, 4 * WIN * WIN), 1) & 15 < WIN
    loads[0].wait()
    spread_rows = [
        jnp.dot(table[b], pick, precision=lax.Precision.HIGHEST, preferred_element_type=F32) for b in range(2)
    ]
    for b in range(2):
        for h in range(HEADS):
            row = jnp.broadcast_to(spread_rows[b][h : h + 1], (WIN, 4 * WIN * WIN))
            rows = jnp.where(
                first_half,
                pltpu.roll(row, 4 * WIN * WIN - WIN + 1, 1, stride=1, stride_axis=0),
                pltpu.roll(row, 1, 1, stride=1, stride_axis=0),
            )
            for y in range(WIN):
                at = (WIN - 1 - y) * 2 * WIN
                piece = rows[:, at : at + 2 * WIN * WIN]
                spot = slice(h * 64 + y * WIN, h * 64 + (y + 1) * WIN)
                if b == 0:
                    bias[0, spot] = piece
                else:
                    row_cut = ((lane >= SHIFT * 2 * WIN) != (y >= SHIFT)) & (gy == ny - 1)
                    bias[1, spot] = piece + jnp.where(col_cut, -100.0, 0.0)
                    bias[2, spot] = piece + jnp.where(col_cut | row_cut, -100.0, 0.0)

    token = lax.broadcasted_iota(jnp.int32, (2 * WIN * WIN, C), 0)
    second = token & 15 >= WIN
    channel = lax.broadcasted_iota(jnp.int32, (1, C), 1)
    heads = [jnp.where(channel >> 5 == h, 1.0, 0.0).astype(BF16) for h in range(HEADS)]
    bands = height // WIN
    band = 2 * WIN * WIN
    group = GROUP
    groups = bands // group
    tall = group * WIN

    def dot(a, b):
        return jnp.dot(a, b, preferred_element_type=F32)

    wide = 2 * group

    def spots(first_band, count):
        return [lax.rem(first_band + k, bands) for k in range(count)]

    def ffn(z, b):
        normed = layer_norm(z, hgain[b : b + 1]).astype(BF16)
        hidden = gelu(dot(normed, ew[b])).astype(BF16)
        return z + dot(hidden, sw[b])

    def block0(i, carry):
        places = spots(i * wide, wide)
        z = jnp.concatenate(
            [feat[pl.ds(r * WIN, WIN), pl.ds(0, 2 * WIN), :].reshape(band, C) for r in places], axis=0
        ).astype(F32)
        triple = dot(layer_norm(z, again[0:1]).astype(BF16), tw[0])
        ctx = [window_pair(triple[k * band : (k + 1) * band], bias[0], second, heads) for k in range(wide)]
        branch = dot(jnp.concatenate(ctx, axis=0), ow[0]).astype(BF16).astype(F32)
        z = ffn(z + branch, 0)
        normed = layer_norm(z, again[1:2])
        for k, r in enumerate(places):
            spot = (pl.ds(r * WIN, WIN), pl.ds(0, 2 * WIN), slice(None))
            first[spot] = z[k * band : (k + 1) * band].reshape(WIN, 2 * WIN, C)
            ext[spot] = normed[k * band : (k + 1) * band].reshape(WIN, 2 * WIN, C)
        return carry

    def remote(src, dst, k, who):
        return pltpu.make_async_remote_copy(
            src_ref=src, dst_ref=dst, send_sem=ssem.at[k], recv_sem=rsem.at[k],
            device_id=who, device_id_type=pl.DeviceIdType.MESH,
        )

    def column(g):
        return remote(cs.at[g], cr.at[g], g, (gy, left))

    def column_back(g):
        return remote(bcs.at[g], bcr.at[g], groups + g, (gy, right))

    strips = [
        remote(rs, rr, 2 * groups, (up, gx)), remote(ds, dr, 2 * groups + 1, (up, left)),
        remote(brs, brr, 2 * groups + 2, (down, gx)), remote(bds, bdr, 2 * groups + 3, (down, right)),
    ]
    half = tall // 2

    def pack(ref, r0, c0):
        low = ref[pl.ds(r0, half), c0 : c0 + SHIFT, :]
        high = ref[pl.ds(r0 + half, half), c0 : c0 + SHIFT, :]
        return jnp.concatenate([low, high], axis=1).reshape(half * WIN, C).astype(BF16)

    def unpack(ref, r0, c0, buf):
        both = buf.astype(F32).reshape(half, WIN, C)
        ref[pl.ds(r0, half), c0 : c0 + SHIFT, :] = both[:, :SHIFT]
        ref[pl.ds(r0 + half, half), c0 : c0 + SHIFT, :] = both[:, SHIFT:]

    for load in loads[1:]:
        load.wait()

    def step0(i, carry):
        block0(i, carry)
        for k in range(2):
            cs[2 * i + k] = pack(ext, (2 * i + k) * tall, 0)

        @pl.when(i == 0)
        def _():
            rs[...] = ext[0:SHIFT, 0:breadth, :].reshape(SHIFT * breadth, C).astype(BF16)
            ds[...] = ext[0:SHIFT, 0:WIN, :].reshape(SHIFT * WIN, C).astype(BF16)
            pl.semaphore_wait(barrier, 6)
            strips[0].start()
            strips[1].start()

        for k in range(2):
            column(2 * i + k).start()
        return carry

    lax.fori_loop(0, groups // 2, step0, 0)

    def block1(i, carry):
        places = spots(i * group, group)
        x = jnp.concatenate(
            [
                ext[pl.ds(r * WIN + SHIFT, WIN), pl.ds(SHIFT, 2 * WIN), :].reshape(band, C)
                for r in places
            ],
            axis=0,
        ).astype(BF16)
        triple = dot(x, tw[1])
        ctx = [
            window_pair(
                triple[k * band : (k + 1) * band],
                bias[jnp.where(r == bands - 1, 2, 1)],
                second, heads,
            )
            for k, r in enumerate(places)
        ]
        branch = dot(jnp.concatenate(ctx, axis=0), ow[1])
        for k, r in enumerate(places):
            back[pl.ds(r * WIN + SHIFT, WIN), pl.ds(SHIFT, 2 * WIN), :] = branch[
                k * band : (k + 1) * band
            ].reshape(WIN, 2 * WIN, C)
        return carry

    def enter(g):
        column(g).wait()
        unpack(ext, g * tall, breadth, cr[g])

    def step1(g, carry):
        @pl.when(g == 0)
        def _():
            enter(g)

        @pl.when(g < groups - 1)
        def _():
            enter(g + 1)

        @pl.when(g == groups - 1)
        def _():
            strips[0].wait()
            strips[1].wait()
            ext[height : height + SHIFT, 0:breadth, :] = rr[...].astype(F32).reshape(SHIFT, breadth, C)
            ext[height : height + SHIFT, breadth : breadth + SHIFT, :] = (
                dr[...].astype(F32).reshape(SHIFT, WIN, C)[:, :SHIFT]
            )

        block1(g, carry)
        bcs[g] = pack(back, g * tall + SHIFT, breadth)
        column_back(g).start()

        @pl.when(g == groups - 1)
        def _():
            brs[...] = back[height : height + SHIFT, 0:breadth, :].reshape(SHIFT * breadth, C).astype(BF16)
            bds[...] = (
                back[height : height + SHIFT, breadth : breadth + WIN, :].reshape(SHIFT * WIN, C).astype(BF16)
            )
            strips[2].start()
            strips[3].start()

        return carry

    lax.fori_loop(0, groups, step1, 0)

    def arrive(g):
        column_back(g).wait()
        unpack(back, g * tall + SHIFT, 0, bcr[g])

    def tail(i, carry):
        places = spots(i * wide + group, wide)
        z = jnp.concatenate(
            [
                (
                    first[pl.ds(r * WIN, WIN), pl.ds(0, 2 * WIN), :]
                    + back[pl.ds(r * WIN, WIN), pl.ds(0, 2 * WIN), :].astype(BF16).astype(F32)
                ).reshape(band, C)
                for r in places
            ],
            axis=0,
        )
        z = ffn(z, 1)
        for k, r in enumerate(places):
            out[pl.ds(r * WIN, WIN), pl.ds(0, 2 * WIN), :] = z[k * band : (k + 1) * band].reshape(
                WIN, 2 * WIN, C
            )
        return carry

    def step2(i, carry):
        @pl.when(i == 0)
        def _():
            arrive(0)

        arrive(2 * i + 1)

        @pl.when(i < groups // 2 - 1)
        def _():
            arrive(2 * i + 2)

        @pl.when(i == groups // 2 - 1)
        def _():
            strips[2].wait()
            strips[3].wait()
            back[0:SHIFT, 0:breadth, :] = brr[...].astype(F32).reshape(SHIFT, breadth, C)
            back[0:SHIFT, 0:SHIFT, :] = bdr[...].astype(F32).reshape(SHIFT, WIN, C)[:, :SHIFT]

        tail(i, carry)
        return carry

    lax.fori_loop(0, groups // 2, step2, 0)


def on_device(ny, nx, *operands):
    height, breadth, _ = operands[0].shape
    groups = height // (GROUP * WIN)
    col, row, corner = (groups, GROUP * WIN * SHIFT, C), (SHIFT * breadth, C), (SHIFT * WIN, C)
    hbm = pl.BlockSpec(memory_space=pl.ANY)
    return pl.pallas_call(
        functools.partial(kernel, ny, nx, height, breadth),
        out_shape=pltpu.VMEM((height, breadth, C), F32),
        in_specs=[hbm] * len(operands),
        out_specs=pl.BlockSpec(memory_space=pltpu.VMEM),
        scratch_shapes=[pltpu.VMEM(x.shape, x.dtype) for x in operands]
        + [
            pltpu.VMEM((height, breadth, C), F32),
            pltpu.VMEM((height + SHIFT, breadth + WIN, C), F32),
            pltpu.VMEM((height + SHIFT, breadth + WIN, C), F32),
            pltpu.VMEM((3, HEADS * WIN * WIN, 2 * WIN * WIN), F32),
        ]
        + [pltpu.VMEM(shape, BF16) for shape in [col] * 4 + [row] * 4 + [corner] * 4]
        + [
            pltpu.SemaphoreType.DMA((2 * groups + 4,)),
            pltpu.SemaphoreType.DMA((2 * groups + 4,)),
            pltpu.SemaphoreType.DMA((len(operands),)),
        ],
        compiler_params=pltpu.CompilerParams(
            collective_id=0, has_side_effects=True, vmem_limit_bytes=(64 * 1024 - 600) * 1024
        ),
        cost_estimate=pl.CostEstimate(flops=10**9, bytes_accessed=2 * 10**6, transcendentals=10**6),
    )(*operands)


def solution(mesh):
    return jax.shard_map(
        functools.partial(on_device, mesh.shape["gy"], mesh.shape["gx"]),
        mesh=mesh,
        in_specs=(P("gy", "gx", None), P(), P(), P(), P(), P(), P(), P()),
        out_specs=P("gy", "gx", None),
        check_vma=False,
    )
```

```python
import functools

import jax
import jax.numpy as jnp
from jax import lax
from jax.experimental import pallas as pl
from jax.experimental.pallas import tpu as pltpu
from jax.sharding import PartitionSpec as P

C = 128
HEADS = 4
WIN = 8
HD = 32
SHIFT = 4
EPSILON = 1e-05
F32 = jnp.float32
BF16 = jnp.bfloat16
GROUP = 2


def layer_norm(values, gain):
    center = values - jnp.mean(values, axis=-1, keepdims=True)
    spread = jnp.mean(center * center, axis=-1, keepdims=True)
    return center * lax.rsqrt(spread + EPSILON) * gain


ERFC = (0.254829592, -0.284496736, 1.421413741, -1.453152027, 1.061405429)
RATE = 0.3275911
POLE = 2**0.5 / RATE
TAIL = [0.5 * c * POLE ** (n + 1) for n, c in enumerate(ERFC)]


def gelu(x):
    a = jnp.abs(x)
    d = a + POLE
    t = pl.reciprocal(d, approx=True)
    t = t * (2.0 - d * t)
    poly = TAIL[4] * t + TAIL[3]
    for coef in TAIL[2::-1]:
        poly = poly * t + coef
    gauss = jnp.exp2((x * x) * (-0.5 * 1.4426950408889634))
    return jnp.maximum(x, 0.0) - (a * t) * (poly * gauss)


def window_pair(triple, turned, bias, second, rows_second, heads):
    triple = triple.reshape(WIN, 2 * WIN, 3 * C)
    zero = jnp.zeros_like(turned)
    query = jnp.concatenate(
        [jnp.where(second, zero, turned), jnp.where(second, turned, zero)], axis=0
    ).astype(BF16)
    keys, values = [], []
    for w in range(2):
        part = triple[:, w * WIN : (w + 1) * WIN, C:].reshape(WIN * WIN, 2 * C).astype(BF16)
        keys.append(jnp.concatenate([part[:, :C] * m for m in heads], axis=0))
        values.append(jnp.concatenate([part[:, C:] * m for m in heads], axis=0))
    keys = jnp.concatenate(keys, axis=1)
    values = jnp.concatenate(values, axis=1)
    scores = jnp.dot(keys, query, preferred_element_type=F32)
    scores = (scores * HD ** (-0.5) + bias).reshape(HEADS, WIN * WIN, 2 * WIN * WIN)
    powers = jnp.exp(scores - jnp.max(scores, axis=1, keepdims=True))
    probs = powers * (1.0 / jnp.sum(powers, axis=1, keepdims=True))
    probs = probs.reshape(HEADS * WIN * WIN, 2 * WIN * WIN).astype(BF16)
    both = lax.dot_general(probs, values, (((0,), (0,)), ((), ())), preferred_element_type=F32)
    return jnp.where(rows_second, both[:, C:], both[:, :C]).astype(BF16)


def kernel(
    ny, nx, height, breadth,
    feat_in, again_in, tw_in, ow_in, table_in, hgain_in, ew_in, sw_in, out,
    feat, again, tw, ow, table, hgain, ew, sw,
    first, ext, back, bias, cs, cr, bcs, bcr, rs, rr, brs, brr, ds, dr, bds, bdr,
    ssem, rsem, isem,
):
    loads = [
        pltpu.make_async_copy(src, dst, isem.at[k])
        for k, (src, dst) in enumerate(
            [
                (table_in, table), (feat_in, feat), (again_in, again), (tw_in, tw),
                (ow_in, ow), (hgain_in, hgain), (ew_in, ew), (sw_in, sw),
            ]
        )
    ]
    for load in loads:
        load.start()
    gy, gx = lax.axis_index("gy"), lax.axis_index("gx")
    up, down = lax.rem(gy + ny - 1, ny), lax.rem(gy + 1, ny)
    left, right = lax.rem(gx + nx - 1, nx), lax.rem(gx + 1, nx)
    barrier = pltpu.get_barrier_semaphore()
    around = [(up, gx), (gy, left), (up, left), (down, gx), (gy, right), (down, right)]
    for who in around:
        pl.semaphore_signal(barrier, inc=1, device_id=who, device_id_type=pl.DeviceIdType.MESH)

    jj = lax.broadcasted_iota(jnp.int32, (WIN, 2 * WIN * WIN), 0)
    lane = lax.broadcasted_iota(jnp.int32, (WIN, 2 * WIN * WIN), 1)
    col_cut = ((jj >= SHIFT) != (lane & 7 >= SHIFT)) & (lane & 15 >= WIN) & (gx == nx - 1)
    extent = 2 * WIN - 1
    entry = lax.broadcasted_iota(jnp.int32, (extent * extent, 4 * WIN * WIN), 0)
    place = lax.broadcasted_iota(jnp.int32, (extent * extent, 4 * WIN * WIN), 1)
    pick = jnp.where(
        (entry == (place >> 4) * extent + (place & 15)) & ((place & 15) < extent), 1.0, 0.0
    )
    first_half = lax.broadcasted_iota(jnp.int32, (WIN, 4 * WIN * WIN), 1) & 15 < WIN
    loads[0].wait()
    spread_rows = [
        jnp.dot(table[b], pick, precision=lax.Precision.HIGHEST, preferred_element_type=F32) for b in range(2)
    ]
    for b in range(2):
        for h in range(HEADS):
            row = jnp.broadcast_to(spread_rows[b][h : h + 1], (WIN, 4 * WIN * WIN))
            rows = jnp.where(
                first_half,
                pltpu.roll(row, 4 * WIN * WIN - WIN + 1, 1, stride=1, stride_axis=0),
                pltpu.roll(row, 1, 1, stride=1, stride_axis=0),
            )
            for y in range(WIN):
                at = (WIN - 1 - y) * 2 * WIN
                piece = rows[:, at : at + 2 * WIN * WIN]
                spot = slice(h * 64 + y * WIN, h * 64 + (y + 1) * WIN)
                if b == 0:
                    bias[0, spot] = piece
                else:
                    row_cut = ((lane >= SHIFT * 2 * WIN) != (y >= SHIFT)) & (gy == ny - 1)
                    bias[1, spot] = piece + jnp.where(col_cut, -100.0, 0.0)
                    bias[2, spot] = piece + jnp.where(col_cut | row_cut, -100.0, 0.0)

    token = lax.broadcasted_iota(jnp.int32, (2 * WIN * WIN, C), 0)
    rows_second = token & 15 >= WIN
    second = lax.broadcasted_iota(jnp.int32, (C, 2 * WIN * WIN), 1) & 15 >= WIN
    channel = lax.broadcasted_iota(jnp.int32, (1, C), 1)
    heads = [jnp.where(channel >> 5 == h, 1.0, 0.0).astype(BF16) for h in range(HEADS)]
    bands = height // WIN
    band = 2 * WIN * WIN
    group = GROUP
    groups = bands // group
    tall = group * WIN

    def dot(a, b):
        return jnp.dot(a, b, preferred_element_type=F32)

    wide = 2 * group

    def spots(first_band, count):
        return [lax.rem(first_band + k, bands) for k in range(count)]

    def ffn(z, b):
        normed = layer_norm(z, hgain[b : b + 1]).astype(BF16)
        hidden = gelu(dot(normed, ew[b])).astype(BF16)
        return z + dot(hidden, sw[b])

    def block0(i, carry):
        places = spots(i * wide, wide)
        z = jnp.concatenate(
            [feat[pl.ds(r * WIN, WIN), pl.ds(0, 2 * WIN), :].reshape(band, C) for r in places], axis=0
        ).astype(F32)
        triple = dot(layer_norm(z, again[0:1]).astype(BF16), tw[0])
        turned = triple[:, :C].T
        ctx = [
            window_pair(
                triple[k * band : (k + 1) * band], turned[:, k * band : (k + 1) * band], bias[0],
                second, rows_second, heads,
            )
            for k in range(wide)
        ]
        branch = dot(jnp.concatenate(ctx, axis=0), ow[0]).astype(BF16).astype(F32)
        z = ffn(z + branch, 0)
        normed = layer_norm(z, again[1:2])
        for k, r in enumerate(places):
            spot = (pl.ds(r * WIN, WIN), pl.ds(0, 2 * WIN), slice(None))
            first[spot] = z[k * band : (k + 1) * band].reshape(WIN, 2 * WIN, C)
            ext[spot] = normed[k * band : (k + 1) * band].reshape(WIN, 2 * WIN, C)
        return carry

    def remote(src, dst, k, who):
        return pltpu.make_async_remote_copy(
            src_ref=src, dst_ref=dst, send_sem=ssem.at[k], recv_sem=rsem.at[k],
            device_id=who, device_id_type=pl.DeviceIdType.MESH,
        )

    def column(g):
        return remote(cs.at[g], cr.at[g], g, (gy, left))

    def column_back(g):
        return remote(bcs.at[g], bcr.at[g], groups + g, (gy, right))

    strips = [
        remote(rs, rr, 2 * groups, (up, gx)), remote(ds, dr, 2 * groups + 1, (up, left)),
        remote(brs, brr, 2 * groups + 2, (down, gx)), remote(bds, bdr, 2 * groups + 3, (down, right)),
    ]
    half = tall // 2

    def pack(ref, r0, c0):
        low = ref[pl.ds(r0, half), c0 : c0 + SHIFT, :]
        high = ref[pl.ds(r0 + half, half), c0 : c0 + SHIFT, :]
        return jnp.concatenate([low, high], axis=1).reshape(half * WIN, C).astype(BF16)

    def unpack(ref, r0, c0, buf):
        both = buf.astype(F32).reshape(half, WIN, C)
        ref[pl.ds(r0, half), c0 : c0 + SHIFT, :] = both[:, :SHIFT]
        ref[pl.ds(r0 + half, half), c0 : c0 + SHIFT, :] = both[:, SHIFT:]

    for load in loads[1:]:
        load.wait()

    def step0(i, carry):
        block0(i, carry)
        for k in range(2):
            cs[2 * i + k] = pack(ext, (2 * i + k) * tall, 0)

        @pl.when(i == 0)
        def _():
            rs[...] = ext[0:SHIFT, 0:breadth, :].reshape(SHIFT * breadth, C).astype(BF16)
            ds[...] = ext[0:SHIFT, 0:WIN, :].reshape(SHIFT * WIN, C).astype(BF16)
            pl.semaphore_wait(barrier, 6)
            strips[0].start()
            strips[1].start()

        for k in range(2):
            column(2 * i + k).start()
        return carry

    lax.fori_loop(0, groups // 2, step0, 0)

    def block1(i, carry):
        places = spots(i * group, group)
        x = jnp.concatenate(
            [
                ext[pl.ds(r * WIN + SHIFT, WIN), pl.ds(SHIFT, 2 * WIN), :].reshape(band, C)
                for r in places
            ],
            axis=0,
        ).astype(BF16)
        triple = dot(x, tw[1])
        turned = triple[:, :C].T
        ctx = [
            window_pair(
                triple[k * band : (k + 1) * band], turned[:, k * band : (k + 1) * band],
                bias[jnp.where(r == bands - 1, 2, 1)], second, rows_second, heads,
            )
            for k, r in enumerate(places)
        ]
        branch = dot(jnp.concatenate(ctx, axis=0), ow[1])
        for k, r in enumerate(places):
            back[pl.ds(r * WIN + SHIFT, WIN), pl.ds(SHIFT, 2 * WIN), :] = branch[
                k * band : (k + 1) * band
            ].reshape(WIN, 2 * WIN, C)
        return carry

    def enter(g):
        column(g).wait()
        unpack(ext, g * tall, breadth, cr[g])

    def step1(g, carry):
        @pl.when(g == 0)
        def _():
            enter(g)

        @pl.when(g < groups - 1)
        def _():
            enter(g + 1)

        @pl.when(g == groups - 1)
        def _():
            strips[0].wait()
            strips[1].wait()
            ext[height : height + SHIFT, 0:breadth, :] = rr[...].astype(F32).reshape(SHIFT, breadth, C)
            ext[height : height + SHIFT, breadth : breadth + SHIFT, :] = (
                dr[...].astype(F32).reshape(SHIFT, WIN, C)[:, :SHIFT]
            )

        block1(g, carry)
        bcs[g] = pack(back, g * tall + SHIFT, breadth)
        column_back(g).start()

        @pl.when(g == groups - 1)
        def _():
            brs[...] = back[height : height + SHIFT, 0:breadth, :].reshape(SHIFT * breadth, C).astype(BF16)
            bds[...] = (
                back[height : height + SHIFT, breadth : breadth + WIN, :].reshape(SHIFT * WIN, C).astype(BF16)
            )
            strips[2].start()
            strips[3].start()

        return carry

    lax.fori_loop(0, groups, step1, 0)

    def arrive(g):
        column_back(g).wait()
        unpack(back, g * tall + SHIFT, 0, bcr[g])

    def tail(i, carry):
        places = spots(i * wide + group, wide)
        z = jnp.concatenate(
            [
                (
                    first[pl.ds(r * WIN, WIN), pl.ds(0, 2 * WIN), :]
                    + back[pl.ds(r * WIN, WIN), pl.ds(0, 2 * WIN), :].astype(BF16).astype(F32)
                ).reshape(band, C)
                for r in places
            ],
            axis=0,
        )
        z = ffn(z, 1)
        for k, r in enumerate(places):
            out[pl.ds(r * WIN, WIN), pl.ds(0, 2 * WIN), :] = z[k * band : (k + 1) * band].reshape(
                WIN, 2 * WIN, C
            )
        return carry

    def step2(i, carry):
        @pl.when(i == 0)
        def _():
            arrive(0)

        arrive(2 * i + 1)

        @pl.when(i < groups // 2 - 1)
        def _():
            arrive(2 * i + 2)

        @pl.when(i == groups // 2 - 1)
        def _():
            strips[2].wait()
            strips[3].wait()
            back[0:SHIFT, 0:breadth, :] = brr[...].astype(F32).reshape(SHIFT, breadth, C)
            back[0:SHIFT, 0:SHIFT, :] = bdr[...].astype(F32).reshape(SHIFT, WIN, C)[:, :SHIFT]

        tail(i, carry)
        return carry

    lax.fori_loop(0, groups // 2, step2, 0)


def on_device(ny, nx, *operands):
    height, breadth, _ = operands[0].shape
    groups = height // (GROUP * WIN)
    col, row, corner = (groups, GROUP * WIN * SHIFT, C), (SHIFT * breadth, C), (SHIFT * WIN, C)
    hbm = pl.BlockSpec(memory_space=pl.ANY)
    return pl.pallas_call(
        functools.partial(kernel, ny, nx, height, breadth),
        out_shape=pltpu.VMEM((height, breadth, C), F32),
        in_specs=[hbm] * len(operands),
        out_specs=pl.BlockSpec(memory_space=pltpu.VMEM),
        scratch_shapes=[pltpu.VMEM(x.shape, x.dtype) for x in operands]
        + [
            pltpu.VMEM((height, breadth, C), F32),
            pltpu.VMEM((height + SHIFT, breadth + WIN, C), F32),
            pltpu.VMEM((height + SHIFT, breadth + WIN, C), F32),
            pltpu.VMEM((3, HEADS * WIN * WIN, 2 * WIN * WIN), F32),
        ]
        + [pltpu.VMEM(shape, BF16) for shape in [col] * 4 + [row] * 4 + [corner] * 4]
        + [
            pltpu.SemaphoreType.DMA((2 * groups + 4,)),
            pltpu.SemaphoreType.DMA((2 * groups + 4,)),
            pltpu.SemaphoreType.DMA((len(operands),)),
        ],
        compiler_params=pltpu.CompilerParams(
            collective_id=0, has_side_effects=True, vmem_limit_bytes=(64 * 1024 - 600) * 1024
        ),
        cost_estimate=pl.CostEstimate(flops=10**9, bytes_accessed=2 * 10**6, transcendentals=10**6),
    )(*operands)


def solution(mesh):
    return jax.shard_map(
        functools.partial(on_device, mesh.shape["gy"], mesh.shape["gx"]),
        mesh=mesh,
        in_specs=(P("gy", "gx", None), P(), P(), P(), P(), P(), P(), P()),
        out_specs=P("gy", "gx", None),
        check_vma=False,
    )
```

```python
import functools

import jax
import jax.numpy as jnp
from jax import lax
from jax.experimental import pallas as pl
from jax.experimental.pallas import tpu as pltpu
from jax.sharding import PartitionSpec as P

C = 128
HEADS = 4
WIN = 8
HD = 32
SHIFT = 4
EPSILON = 1e-05
F32 = jnp.float32
BF16 = jnp.bfloat16
GROUP = 2


def layer_norm(values, gain):
    center = values - jnp.mean(values, axis=-1, keepdims=True)
    spread = jnp.mean(center * center, axis=-1, keepdims=True)
    return center * lax.rsqrt(spread + EPSILON) * gain


ERFC = (0.254829592, -0.284496736, 1.421413741, -1.453152027, 1.061405429)
RATE = 0.3275911
POLE = 2**0.5 / RATE
TAIL = [0.5 * c * POLE ** (n + 1) for n, c in enumerate(ERFC)]


def gelu(x):
    a = jnp.abs(x)
    d = a + POLE
    t = pl.reciprocal(d, approx=True)
    t = t * (2.0 - d * t)
    poly = TAIL[4] * t + TAIL[3]
    for coef in TAIL[2::-1]:
        poly = poly * t + coef
    gauss = jnp.exp2((x * x) * (-0.5 * 1.4426950408889634))
    return jnp.maximum(x, 0.0) - (a * t) * (poly * gauss)


def window_pair(triple, bias, second, heads):
    triple = triple.reshape(WIN, 2 * WIN, 3 * C)
    query = triple[:, :, :C].reshape(2 * WIN * WIN, C)
    zero = jnp.zeros_like(query)
    query = jnp.concatenate(
        [jnp.where(second, zero, query), jnp.where(second, query, zero)], axis=1
    ).astype(BF16)
    keys, values = [], []
    for w in range(2):
        part = triple[:, w * WIN : (w + 1) * WIN, C:].reshape(WIN * WIN, 2 * C).astype(BF16)
        keys.append(jnp.concatenate([part[:, :C] * m for m in heads], axis=0))
        values.append(jnp.concatenate([part[:, C:] * m for m in heads], axis=0))
    keys = jnp.concatenate(keys, axis=1)
    values = jnp.concatenate(values, axis=1)
    scores = lax.dot_general(keys, query, (((1,), (1,)), ((), ())), preferred_element_type=F32)
    scores = (scores * HD ** (-0.5) + bias).reshape(HEADS, WIN * WIN, 2 * WIN * WIN)
    powers = jnp.exp(scores - jnp.max(scores, axis=1, keepdims=True))
    probs = powers * (1.0 / jnp.sum(powers, axis=1, keepdims=True))
    probs = probs.reshape(HEADS * WIN * WIN, 2 * WIN * WIN).astype(BF16)
    both = lax.dot_general(probs, values, (((0,), (0,)), ((), ())), preferred_element_type=F32)
    return jnp.where(second, both[:, C:], both[:, :C]).astype(BF16)


def kernel(
    ny, nx, height, breadth,
    feat_in, again_in, tw_in, ow_in, table_in, hgain_in, ew_in, sw_in, out,
    feat, again, tw, ow, table, hgain, ew, sw,
    first, ext, back, bias, cs, cr, bcs, bcr, rs, rr, brs, brr, ds, dr, bds, bdr,
    ssem, rsem, isem,
):
    loads = [
        pltpu.make_async_copy(src, dst, isem.at[k])
        for k, (src, dst) in enumerate(
            [
                (table_in, table), (feat_in, feat), (again_in, again), (tw_in, tw),
                (ow_in, ow), (hgain_in, hgain), (ew_in, ew), (sw_in, sw),
            ]
        )
    ]
    for load in loads:
        load.start()
    gy, gx = lax.axis_index("gy"), lax.axis_index("gx")
    up, down = lax.rem(gy + ny - 1, ny), lax.rem(gy + 1, ny)
    left, right = lax.rem(gx + nx - 1, nx), lax.rem(gx + 1, nx)
    barrier = pltpu.get_barrier_semaphore()
    around = [(up, gx), (gy, left), (up, left), (down, gx), (gy, right), (down, right)]
    for who in around:
        pl.semaphore_signal(barrier, inc=1, device_id=who, device_id_type=pl.DeviceIdType.MESH)

    jj = lax.broadcasted_iota(jnp.int32, (WIN, 2 * WIN * WIN), 0)
    lane = lax.broadcasted_iota(jnp.int32, (WIN, 2 * WIN * WIN), 1)
    col_cut = ((jj >= SHIFT) != (lane & 7 >= SHIFT)) & (lane & 15 >= WIN) & (gx == nx - 1)
    extent = 2 * WIN - 1
    entry = lax.broadcasted_iota(jnp.int32, (extent * extent, 4 * WIN * WIN), 0)
    place = lax.broadcasted_iota(jnp.int32, (extent * extent, 4 * WIN * WIN), 1)
    pick = jnp.where(
        (entry == (place >> 4) * extent + (place & 15)) & ((place & 15) < extent), 1.0, 0.0
    )
    first_half = lax.broadcasted_iota(jnp.int32, (WIN, 4 * WIN * WIN), 1) & 15 < WIN
    loads[0].wait()
    rest = jnp.concatenate([table[0], table[1]], axis=0)
    terms = []
    for _ in range(3):
        terms.append(rest.astype(BF16).astype(F32))
        rest = rest - terms[-1]
    found = jnp.dot(
        jnp.concatenate(terms, axis=0).astype(BF16), pick.astype(BF16), preferred_element_type=F32
    )
    picked = found[:WIN] + found[WIN : 2 * WIN] + found[2 * WIN :]
    for b in range(2):
        for h in range(HEADS):
            row = jnp.broadcast_to(picked[b * HEADS + h : b * HEADS + h + 1], (WIN, 4 * WIN * WIN))
            rows = jnp.where(
                first_half,
                pltpu.roll(row, 4 * WIN * WIN - WIN + 1, 1, stride=1, stride_axis=0),
                pltpu.roll(row, 1, 1, stride=1, stride_axis=0),
            )
            for y in range(WIN):
                at = (WIN - 1 - y) * 2 * WIN
                piece = rows[:, at : at + 2 * WIN * WIN]
                spot = slice(h * 64 + y * WIN, h * 64 + (y + 1) * WIN)
                if b == 0:
                    bias[0, spot] = piece
                else:
                    row_cut = ((lane >= SHIFT * 2 * WIN) != (y >= SHIFT)) & (gy == ny - 1)
                    bias[1, spot] = piece + jnp.where(col_cut, -100.0, 0.0)
                    bias[2, spot] = piece + jnp.where(col_cut | row_cut, -100.0, 0.0)

    token = lax.broadcasted_iota(jnp.int32, (2 * WIN * WIN, C), 0)
    second = token & 15 >= WIN
    channel = lax.broadcasted_iota(jnp.int32, (1, C), 1)
    heads = [jnp.where(channel >> 5 == h, 1.0, 0.0).astype(BF16) for h in range(HEADS)]
    bands = height // WIN
    band = 2 * WIN * WIN
    group = GROUP
    groups = bands // group
    tall = group * WIN

    def dot(a, b):
        return jnp.dot(a, b, preferred_element_type=F32)

    wide = 2 * group

    def spots(first_band, count):
        return [lax.rem(first_band + k, bands) for k in range(count)]

    def ffn(z, b):
        normed = layer_norm(z, hgain[b : b + 1]).astype(BF16)
        hidden = gelu(dot(normed, ew[b])).astype(BF16)
        return z + dot(hidden, sw[b])

    def block0(i, carry):
        places = spots(i * wide, wide)
        z = jnp.concatenate(
            [feat[pl.ds(r * WIN, WIN), pl.ds(0, 2 * WIN), :].reshape(band, C) for r in places], axis=0
        ).astype(F32)
        triple = dot(layer_norm(z, again[0:1]).astype(BF16), tw[0])
        ctx = [window_pair(triple[k * band : (k + 1) * band], bias[0], second, heads) for k in range(wide)]
        branch = dot(jnp.concatenate(ctx, axis=0), ow[0]).astype(BF16).astype(F32)
        z = ffn(z + branch, 0)
        normed = layer_norm(z, again[1:2])
        for k, r in enumerate(places):
            spot = (pl.ds(r * WIN, WIN), pl.ds(0, 2 * WIN), slice(None))
            first[spot] = z[k * band : (k + 1) * band].reshape(WIN, 2 * WIN, C)
            ext[spot] = normed[k * band : (k + 1) * band].reshape(WIN, 2 * WIN, C)
        return carry

    def remote(src, dst, k, who):
        return pltpu.make_async_remote_copy(
            src_ref=src, dst_ref=dst, send_sem=ssem.at[k], recv_sem=rsem.at[k],
            device_id=who, device_id_type=pl.DeviceIdType.MESH,
        )

    def column(g):
        return remote(cs.at[g], cr.at[g], g, (gy, left))

    def column_back(g):
        return remote(bcs.at[g], bcr.at[g], groups + g, (gy, right))

    strips = [
        remote(rs, rr, 2 * groups, (up, gx)), remote(ds, dr, 2 * groups + 1, (up, left)),
        remote(brs, brr, 2 * groups + 2, (down, gx)), remote(bds, bdr, 2 * groups + 3, (down, right)),
    ]
    half = tall // 2

    def pack(ref, r0, c0):
        low = ref[pl.ds(r0, half), c0 : c0 + SHIFT, :]
        high = ref[pl.ds(r0 + half, half), c0 : c0 + SHIFT, :]
        return jnp.concatenate([low, high], axis=1).reshape(half * WIN, C).astype(BF16)

    def unpack(ref, r0, c0, buf):
        both = buf.astype(F32).reshape(half, WIN, C)
        ref[pl.ds(r0, half), c0 : c0 + SHIFT, :] = both[:, :SHIFT]
        ref[pl.ds(r0 + half, half), c0 : c0 + SHIFT, :] = both[:, SHIFT:]

    for load in loads[1:]:
        load.wait()

    def step0(i, carry):
        block0(i, carry)
        for k in range(2):
            cs[2 * i + k] = pack(ext, (2 * i + k) * tall, 0)

        @pl.when(i == 0)
        def _():
            rs[...] = ext[0:SHIFT, 0:breadth, :].reshape(SHIFT * breadth, C).astype(BF16)
            ds[...] = ext[0:SHIFT, 0:WIN, :].reshape(SHIFT * WIN, C).astype(BF16)
            pl.semaphore_wait(barrier, 6)
            strips[0].start()
            strips[1].start()

        for k in range(2):
            column(2 * i + k).start()
        return carry

    lax.fori_loop(0, groups // 2, step0, 0)

    def block1(i, carry):
        places = spots(i * group, group)
        x = jnp.concatenate(
            [
                ext[pl.ds(r * WIN + SHIFT, WIN), pl.ds(SHIFT, 2 * WIN), :].reshape(band, C)
                for r in places
            ],
            axis=0,
        ).astype(BF16)
        triple = dot(x, tw[1])
        ctx = [
            window_pair(
                triple[k * band : (k + 1) * band],
                bias[jnp.where(r == bands - 1, 2, 1)],
                second, heads,
            )
            for k, r in enumerate(places)
        ]
        branch = dot(jnp.concatenate(ctx, axis=0), ow[1])
        for k, r in enumerate(places):
            back[pl.ds(r * WIN + SHIFT, WIN), pl.ds(SHIFT, 2 * WIN), :] = branch[
                k * band : (k + 1) * band
            ].reshape(WIN, 2 * WIN, C)
        return carry

    def enter(g):
        column(g).wait()
        unpack(ext, g * tall, breadth, cr[g])

    def step1(g, carry):
        @pl.when(g == 0)
        def _():
            enter(g)

        @pl.when(g < groups - 1)
        def _():
            enter(g + 1)

        @pl.when(g == groups - 1)
        def _():
            strips[0].wait()
            strips[1].wait()
            ext[height : height + SHIFT, 0:breadth, :] = rr[...].astype(F32).reshape(SHIFT, breadth, C)
            ext[height : height + SHIFT, breadth : breadth + SHIFT, :] = (
                dr[...].astype(F32).reshape(SHIFT, WIN, C)[:, :SHIFT]
            )

        block1(g, carry)
        bcs[g] = pack(back, g * tall + SHIFT, breadth)
        column_back(g).start()

        @pl.when(g == groups - 1)
        def _():
            brs[...] = back[height : height + SHIFT, 0:breadth, :].reshape(SHIFT * breadth, C).astype(BF16)
            bds[...] = (
                back[height : height + SHIFT, breadth : breadth + WIN, :].reshape(SHIFT * WIN, C).astype(BF16)
            )
            strips[2].start()
            strips[3].start()

        return carry

    lax.fori_loop(0, groups, step1, 0)

    def arrive(g):
        column_back(g).wait()
        unpack(back, g * tall + SHIFT, 0, bcr[g])

    def tail(i, carry):
        places = spots(i * wide + group, wide)
        z = jnp.concatenate(
            [
                (
                    first[pl.ds(r * WIN, WIN), pl.ds(0, 2 * WIN), :]
                    + back[pl.ds(r * WIN, WIN), pl.ds(0, 2 * WIN), :].astype(BF16).astype(F32)
                ).reshape(band, C)
                for r in places
            ],
            axis=0,
        )
        z = ffn(z, 1)
        for k, r in enumerate(places):
            out[pl.ds(r * WIN, WIN), pl.ds(0, 2 * WIN), :] = z[k * band : (k + 1) * band].reshape(
                WIN, 2 * WIN, C
            )
        return carry

    def step2(i, carry):
        @pl.when(i == 0)
        def _():
            arrive(0)

        arrive(2 * i + 1)

        @pl.when(i < groups // 2 - 1)
        def _():
            arrive(2 * i + 2)

        @pl.when(i == groups // 2 - 1)
        def _():
            strips[2].wait()
            strips[3].wait()
            back[0:SHIFT, 0:breadth, :] = brr[...].astype(F32).reshape(SHIFT, breadth, C)
            back[0:SHIFT, 0:SHIFT, :] = bdr[...].astype(F32).reshape(SHIFT, WIN, C)[:, :SHIFT]

        tail(i, carry)
        return carry

    lax.fori_loop(0, groups // 2, step2, 0)


def on_device(ny, nx, *operands):
    height, breadth, _ = operands[0].shape
    groups = height // (GROUP * WIN)
    col, row, corner = (groups, GROUP * WIN * SHIFT, C), (SHIFT * breadth, C), (SHIFT * WIN, C)
    hbm = pl.BlockSpec(memory_space=pl.ANY)
    return pl.pallas_call(
        functools.partial(kernel, ny, nx, height, breadth),
        out_shape=pltpu.VMEM((height, breadth, C), F32),
        in_specs=[hbm] * len(operands),
        out_specs=pl.BlockSpec(memory_space=pltpu.VMEM),
        scratch_shapes=[pltpu.VMEM(x.shape, x.dtype) for x in operands]
        + [
            pltpu.VMEM((height, breadth, C), F32),
            pltpu.VMEM((height + SHIFT, breadth + WIN, C), F32),
            pltpu.VMEM((height + SHIFT, breadth + WIN, C), F32),
            pltpu.VMEM((3, HEADS * WIN * WIN, 2 * WIN * WIN), F32),
        ]
        + [pltpu.VMEM(shape, BF16) for shape in [col] * 4 + [row] * 4 + [corner] * 4]
        + [
            pltpu.SemaphoreType.DMA((2 * groups + 4,)),
            pltpu.SemaphoreType.DMA((2 * groups + 4,)),
            pltpu.SemaphoreType.DMA((len(operands),)),
        ],
        compiler_params=pltpu.CompilerParams(
            collective_id=0, has_side_effects=True, vmem_limit_bytes=(64 * 1024 - 600) * 1024
        ),
        cost_estimate=pl.CostEstimate(flops=10**9, bytes_accessed=2 * 10**6, transcendentals=10**6),
    )(*operands)


def solution(mesh):
    return jax.shard_map(
        functools.partial(on_device, mesh.shape["gy"], mesh.shape["gx"]),
        mesh=mesh,
        in_specs=(P("gy", "gx", None), P(), P(), P(), P(), P(), P(), P()),
        out_specs=P("gy", "gx", None),
        check_vma=False,
    )
```
